256 devices in a mesh: ctx: 128 (over x, y, z_lo, core), mp: 2 (over z_hi).
Axes of the slice: x: 4, y: 4, z: 8 (z_hi: 2, z_lo: 4; z = z_hi * 4 + z_lo), core: 2. Of those that a mesh axis runs over, the one named last changes fastest.
Arguments:
- query_rows: bfloat16 [32768, 768], P('ctx', 'mp'), may hold values from -6 to 6
- key_rows: bfloat16 [32768, 768], P('ctx', 'mp'), may hold values from -6 to 6
- value_rows: bfloat16 [32768, 768], P('ctx', 'mp'), may hold values from -6 to 6
- w_output: bfloat16 [768, 768], P('mp'), may hold values from -0.21875 to 0.21875
- grad_output: bfloat16 [32768, 768], P('ctx', 'mp'), may hold values from -6 to 6
Outputs:
- layer_out: bfloat16 [32768, 768], P('ctx', 'mp')
- grad_query: bfloat16 [32768, 768], P('ctx', 'mp')
- grad_key: bfloat16 [32768, 768], P('ctx', 'mp')
- grad_value: bfloat16 [32768, 768], P('ctx', 'mp')
- grad_weight: float32 [768, 768], P('mp')
The draws below stay inside these ranges and needn't reach their ends.
All inputs are finite; a program needn't handle non-finite values.
Results may differ from the reference program's by a relative error of at most 0.0091.
Values may be sent and summed in bfloat16 or wider, within the bound.
A program may use at most 128 MiB of HBM per device.

```python
import jax
import jax.numpy as jnp
from jax import lax

HEADS = 12
HEAD = 64
BLOCK = 64
TOKENS = 32768
LOCAL_LEVELS = 2
CTX_BITS = 7


def layered(key, noise):
    levels = LOCAL_LEVELS + CTX_BITS
    shift = BLOCK.bit_length() - 1
    field = 0.5 * noise
    for level in range(levels):
        span = 1 << shift + level
        coarse = jax.random.normal(jax.random.fold_in(key, 200 + level), (TOKENS // span, HEADS * HEAD), jnp.float32)
        field = field + 0.3 * jnp.repeat(coarse, span, axis=0)
    return jnp.clip(field, -6.0, 6.0)


def draw_query_rows(key, part):
    key = jax.random.fold_in(key, 1)
    base = jnp.clip(jax.random.normal(key, (TOKENS, HEADS * HEAD), jnp.float32), -6.0, 6.0)
    return base.astype(jnp.bfloat16)


def draw_key_rows(key, part):
    key = jax.random.fold_in(key, 2)
    noise = jax.random.normal(key, (TOKENS, HEADS * HEAD), jnp.float32)
    return layered(key, noise).astype(jnp.bfloat16)


def draw_value_rows(key, part):
    key = jax.random.fold_in(key, 3)
    noise = jax.random.normal(key, (TOKENS, HEADS * HEAD), jnp.float32)
    return layered(key, noise).astype(jnp.bfloat16)


def shard_levels(stream_key, dims, cuts, least, high):
    def one(dim, parts):
        draws = jax.random.uniform(jax.random.fold_in(jax.random.fold_in(stream_key, 6), dim), (parts,), jnp.float32, least / len(cuts), high / len(cuts))
        return jnp.repeat(jnp.exp(draws), dims[dim] // parts).reshape((-1,) + (1,) * (len(dims) - dim - 1))

    factor_of = one(*cuts[0])
    for cut in cuts[1:]:
        factor_of = factor_of * one(*cut)
    return factor_of


def normal_values(stream_key, dims, scale, bound, cuts=(), dtype=jnp.bfloat16):
    drawn = jax.random.normal(stream_key, dims, jnp.float32) * scale
    if len(cuts) > 0:
        drawn = shard_levels(stream_key, dims, cuts, -0.22, 0.18) * drawn
    return jnp.clip(drawn, min=-bound, max=bound).astype(dtype)


def setup_inputs(seed: int = 0) -> dict:
    arg_keys = jax.random.split(jax.random.key(seed), 6)
    return {
        "query_rows": draw_query_rows(jax.random.fold_in(arg_keys[5], 71), 0),
        "key_rows": draw_key_rows(jax.random.fold_in(arg_keys[5], 71), 0),
        "value_rows": draw_value_rows(jax.random.fold_in(arg_keys[5], 71), 0),
        "w_output": normal_values(arg_keys[3], (HEADS * HEAD, HEADS * HEAD), (HEADS * HEAD) ** -0.5, 0.21875, ((0, 2),)),
        "grad_output": normal_values(arg_keys[4], (TOKENS, HEADS * HEAD), 1.0, 6.0, ((0, 128), (1, 2))),
    }


def to_low(values):
    return lax.optimization_barrier(values.astype(jnp.bfloat16)).astype(jnp.float32)


def pool_rows(stacked):
    halves = stacked.astype(jnp.float32).reshape((stacked.shape[0], stacked.shape[1] // 2, 2) + stacked.shape[2:])
    return ((halves[:, :, 0] + halves[:, :, 1]) * 0.5).astype(jnp.bfloat16)


def spread_rows(gradient):
    return 0.5 * jnp.repeat(gradient, 2, axis=1)


def flip_groups(grouped):
    shape = grouped.shape
    paired = grouped.reshape((shape[0], shape[1] // 2, 2) + shape[2:])
    return paired[:, :, ::-1].reshape(shape)


def attend(queries, key_sets, grad_attn):
    count, heads_here, head_size = queries.shape
    scale = HEAD ** -0.5
    grouped_list = []
    score_list = []
    for stacked in key_sets:
        groups = stacked.shape[1]
        grouped = queries.reshape(groups, count // groups, heads_here, head_size).astype(jnp.float32)
        grouped_list.append(grouped)
        scores = jnp.einsum("gqhe,gkhe->gqhk", grouped, stacked[0].astype(jnp.float32))
        score_list.append(scores.reshape(count, heads_here, stacked.shape[2]))
    scores = jnp.concatenate(score_list, axis=-1) * scale
    largest = jnp.max(scores, axis=-1, keepdims=True)
    weights = jnp.exp(scores - largest)
    probs = weights / jnp.sum(weights, axis=-1, keepdims=True)
    probs_low = to_low(probs)
    grad_low = to_low(grad_attn)
    width = key_sets[0].shape[2]
    outputs = jnp.zeros(queries.shape, jnp.float32)
    pieces = []
    grad_list = []
    for index, stacked in enumerate(key_sets):
        groups = stacked.shape[1]
        piece = probs_low[:, :, index * width:(index + 1) * width].reshape(groups, count // groups, heads_here, width)
        grad_grouped = grad_low.reshape(groups, count // groups, heads_here, head_size)
        values = stacked[1].astype(jnp.float32)
        pieces.append((piece, grad_grouped))
        outputs = outputs + jnp.einsum("gqhk,gkhe->gqhe", piece, values).reshape(queries.shape)
        grad_list.append(jnp.einsum("gqhe,gkhe->gqhk", grad_grouped, values).reshape(count, heads_here, width))
    grad_probs = jnp.concatenate(grad_list, axis=-1)
    centre = jnp.sum(probs * grad_probs, axis=-1, keepdims=True)
    grad_scores = to_low(probs * (grad_probs - centre) * scale)
    grad_queries = jnp.zeros(queries.shape, jnp.float32)
    grad_sets = []
    for index, stacked in enumerate(key_sets):
        groups = stacked.shape[1]
        piece, grad_grouped = pieces[index]
        grad_piece = grad_scores[:, :, index * width:(index + 1) * width].reshape(groups, count // groups, heads_here, width)
        grad_queries = grad_queries + jnp.einsum("gqhk,gkhe->gqhe", grad_piece, stacked[0].astype(jnp.float32)).reshape(queries.shape)
        grad_keys = jnp.einsum("gqhk,gqhe->gkhe", grad_piece, grouped_list[index])
        grad_values = jnp.einsum("gqhk,gqhe->gkhe", piece, grad_grouped)
        grad_sets.append(jnp.stack([grad_keys, grad_values]))
    return outputs, grad_queries, grad_sets


def one_head(inputs):
    query_head, key_head, value_head, grad_head = inputs
    levels = LOCAL_LEVELS + CTX_BITS
    queries = query_head[:, None, :]
    stacked = jnp.stack([key_head, value_head])[:, :, None, :]
    pyramid = [stacked]
    for level in range(1, levels):
        pyramid.append(pool_rows(pyramid[-1]))
    sets = [stacked.reshape(2, TOKENS // BLOCK, BLOCK, 1, HEAD)]
    for level in range(levels):
        sets.append(flip_groups(pyramid[level].reshape(2, -1, BLOCK, 1, HEAD)))
    outputs, grad_queries, grad_sets = attend(queries, sets, grad_head[:, None, :])
    carried = jnp.zeros((2, 2 * BLOCK, 1, HEAD), jnp.float32)
    for level in reversed(range(levels)):
        level_grad = flip_groups(grad_sets[level + 1]).reshape(2, -1, 1, HEAD)
        if level == levels - 1:
            carried = level_grad
        else:
            carried = level_grad + spread_rows(carried)
    carried = carried + grad_sets[0].reshape(2, TOKENS, 1, HEAD)
    return (outputs[:, 0].astype(jnp.bfloat16), grad_queries[:, 0].astype(jnp.bfloat16),
            carried[0, :, 0].astype(jnp.bfloat16), carried[1, :, 0].astype(jnp.bfloat16))


def heads_first(values):
    return values.reshape(TOKENS, HEADS, HEAD).transpose(1, 0, 2)


def heads_back(values):
    return values.transpose(1, 0, 2).reshape(TOKENS, HEADS * HEAD)


def reference(query_rows, key_rows, value_rows, w_output, grad_output):
    grad_attn = jnp.dot(grad_output, w_output.T, preferred_element_type=jnp.float32)
    attn_heads, query_heads, key_heads, value_heads = lax.map(
        one_head, (heads_first(query_rows), heads_first(key_rows), heads_first(value_rows), heads_first(grad_attn)))
    attn = heads_back(attn_heads)
    layer_out = jnp.dot(attn, w_output, preferred_element_type=jnp.float32).astype(jnp.bfloat16)
    grad_weight = jnp.dot(attn.T, grad_output, preferred_element_type=jnp.float32)
    return layer_out, heads_back(query_heads), heads_back(key_heads), heads_back(value_heads), grad_weight
```

```python
import functools

import jax
import jax.numpy as jnp
from jax import lax
from jax.experimental import pallas as pl
from jax.experimental.pallas import tpu as pltpu
from jax.sharding import PartitionSpec as P

HEAD = 64
BLOCK = 64
NEAR = 8
NEAR_BITS = 3
MESH = pl.DeviceIdType.MESH
BF = jnp.bfloat16
F32 = jnp.float32


def iota(shape, axis):
    return lax.broadcasted_iota(jnp.int32, shape, axis)


def where_one(condition, weight):
    return jnp.where(condition, weight, 0.0).astype(BF)


def mm(a, b):
    return jnp.dot(a, b, preferred_element_type=F32)


def mm_nt(a, b):
    return lax.dot_general(a, b, (((1,), (1,)), ((), ())), preferred_element_type=F32)


def pool(rows):
    count = rows.shape[0]
    out = max(count // 2, 16)
    halves = where_one(iota((out, count), 1) // 2 == iota((out, count), 0), 0.5)
    return mm(halves, rows).astype(BF)


def sibling(index):
    return index + 1 - 2 * (index % 2)


def kernel(
    hi_bits,
    q_ref, k_ref, v_ref, w_ref, go_ref,
    lo_out, dq_out, dk_out, dv_out, gw_out,
    near_rows, level1, far, far_f32, ug, up, up_f32, fg, bdq, bdo, probs, attn_t, dq_t,
    d_far, d_send, d_f32, r1_land, r1_f32, msg, r2_land, d_loc, d_l1,
    gw_send, gw_land, gw_part, gw_ar, gw_all, lo_send, lo_land,
    f1_s, f1_r, f1u_s, f1u_r, f2_s, f2_r, r1_s, r1_r, r1g_s, r1g_r,
    r2_s, r2_r, r2g_s, r2g_r, ag_s, ag_r, mp_s, mp_r,
):
    his = 1 << hi_bits
    sets = NEAR_BITS + hi_bits
    keys = sets * BLOCK
    wide = 2 * 384
    place = lax.axis_index("ctx")
    mp = lax.axis_index("mp")
    hi = place // NEAR
    lo = place % NEAR

    def near_id(e):
        return (hi * NEAR + e, mp)

    def far_id(f):
        return (f * NEAR + lo, mp)

    mp_id = (place, 1 - mp)

    def near_copy(b, j, src, dst, send, recv):
        n = 1 << b
        e = sibling(lo // n) * n + j
        return pltpu.make_async_remote_copy(
            src_ref=src, dst_ref=dst, send_sem=send.at[n - 1 + j], recv_sem=recv.at[n - 1 + lo % n],
            device_id=near_id(e), device_id_type=MESH)

    def far_copy(b, j, src, dst, send, recv):
        n = 1 << b
        f = sibling(hi // n) * n + j
        return pltpu.make_async_remote_copy(
            src_ref=src, dst_ref=dst, send_sem=send.at[n - 1 + j], recv_sem=recv.at[n - 1 + hi % n],
            device_id=far_id(f), device_id_type=MESH)

    def each(n, mine, body):
        if n == 1:
            body(0)
        else:
            def step(t, c):
                body((t + mine) % n)
                return c
            lax.fori_loop(0, n, step, 0)

    def wait_in(dst, recv):
        pltpu.make_async_copy(dst, dst, recv).wait()

    barrier = pltpu.get_barrier_semaphore()
    for b in range(NEAR_BITS):
        n = 1 << b
        each(n, lo, lambda j, n=n: pl.semaphore_signal(
            barrier, inc=1, device_id=near_id(sibling(lo // n) * n + j), device_id_type=MESH))
    for b in range(hi_bits):
        n = 1 << b
        each(n, hi, lambda j, n=n: pl.semaphore_signal(
            barrier, inc=1, device_id=far_id(sibling(hi // n) * n + j), device_id_type=MESH))
    pl.semaphore_signal(barrier, inc=1, device_id=mp_id, device_id_type=MESH)

    rows = jnp.concatenate([k_ref[...], v_ref[...]], axis=1)
    rows = pool(rows)
    level1[...] = rows
    rows = pool(rows)
    near_rows[0:64, :] = rows
    rows = pool(rows)
    near_rows[64:96, :] = rows
    rows = pool(rows)
    near_rows[96:112, :] = rows
    first = pool(rows)
    step_up = where_one(iota((16, 16), 1) // 2 + 8 == iota((16, 16), 0), 0.5)
    upper = first
    for _ in range(3):
        upper = (first.astype(F32) + mm(step_up, upper)).astype(BF)
    near_rows[112:128, :] = upper
    ug[lo] = upper
    fg[mp] = go_ref[...]

    pl.semaphore_wait(barrier, NEAR - 1 + his - 1 + 1)

    near_at = (0, 64, 96)

    for b in range(NEAR_BITS):
        n, r = 1 << b, BLOCK >> b
        each(n, lo, lambda j, b=b: near_copy(
            b, j, near_rows.at[pl.ds(112, 16)], ug.at[lo], f1u_s, f1u_r).start())
    for b in range(NEAR_BITS):
        n, r = 1 << b, BLOCK >> b
        each(n, lo, lambda j, b=b, n=n, r=r: near_copy(
            b, j, near_rows.at[pl.ds(near_at[b], r)],
            far.at[pl.ds(pl.multiple_of(b * BLOCK + (lo % n) * r, 16), r)], f1_s, f1_r).start())

    lane_low = iota((128, 128), 1) < HEAD
    masks = (where_one(lane_low, 1.0), where_one(jnp.logical_not(lane_low), 1.0))

    def local_rows(own, i, p, side):
        lanes = slice(i * 128, i * 128 + 128)
        upper_lanes = slice(side * 384 + i * 128, side * 384 + i * 128 + 128)
        return jnp.concatenate(
            [own[p * 128:p * 128 + 128, lanes], level1[64 * (1 - p):64 * (1 - p) + 64, upper_lanes]], axis=0)

    for i in range(3):
        for p in range(2):
            part = q_ref[p * 128:p * 128 + 128, i * 128:i * 128 + 128]
            for h in range(2):
                at = p * 256 + h * 128
                bdq[i, at:at + 128, :] = part * masks[h]
        for p in range(2):
            probs[i, keys:keys + 192, p * 256:p * 256 + 256] = mm_nt(
                local_rows(k_ref, i, p, 0), bdq[i, p * 256:p * 256 + 256, :])

    for b in range(NEAR_BITS):
        n = 1 << b
        each(n, lo, lambda j, n=n: wait_in(
            ug.at[sibling(lo // n) * n + j], f1u_r.at[n - 1 + j]))
    gathered = ug[...].reshape(NEAR * 16, wide)
    a = iota((128, 128), 0)
    source = jnp.where(
        a < 64, a // 8 * 16 + a % 8,
        jnp.where(a < 96, (a - 64) // 4 * 16 + 8 + a % 4,
                  jnp.where(a < 112, (a - 96) // 2 * 16 + 12 + a % 2, (a - 112) * 16 + 14)))
    levels = mm(where_one(iota((128, 128), 1) == source, 1.0), gathered)
    up[...] = levels[0:112].astype(BF)
    up_f32[...] = levels[112:120]

    up_at = (0, 64, 96)
    for b in reversed(range(hi_bits)):
        n, r = 1 << b, BLOCK >> b
        if b < 3:
            each(n, hi, lambda j, b=b, n=n, r=r: far_copy(
                b, j, up.at[pl.ds(up_at[b], r)],
                far.at[pl.ds(pl.multiple_of((NEAR_BITS + b) * BLOCK + (hi % n) * r, 16), r)], f2_s, f2_r).start())
        else:
            each(n, hi, lambda j, b=b, n=n, r=r: far_copy(
                b, j, up_f32, far_f32.at[pl.ds(pl.multiple_of((hi % n) * r, 8), r)], f2_s, f2_r).start())
    to_mp = pltpu.make_async_remote_copy(
        src_ref=go_ref, dst_ref=fg.at[mp], send_sem=mp_s.at[0], recv_sem=mp_r.at[0],
        device_id=mp_id, device_id_type=MESH)
    to_mp.start()

    for b in range(NEAR_BITS):
        n, r = 1 << b, BLOCK >> b
        each(n, lo, lambda j, b=b, n=n, r=r: wait_in(
            far.at[pl.ds(pl.multiple_of(b * BLOCK + j * r, 16), r)], f1_r.at[n - 1 + j]))
    for i in range(3):
        probs[i, 0:192, :] = mm_nt(far[0:192, i * 128:i * 128 + 128], bdq[i])

    for b in range(hi_bits):
        n, r = 1 << b, BLOCK >> b
        if b < 3:
            each(n, hi, lambda j, b=b, n=n, r=r: wait_in(
                far.at[pl.ds(pl.multiple_of((NEAR_BITS + b) * BLOCK + j * r, 16), r)], f2_r.at[n - 1 + j]))
        else:
            each(n, hi, lambda j, b=b, n=n, r=r: wait_in(
                far_f32.at[pl.ds(pl.multiple_of(j * r, 8), r)], f2_r.at[n - 1 + j]))
            far[6 * BLOCK:7 * BLOCK, :] = far_f32[...].astype(BF)

    unit = HEAD ** -0.5 * 1.4426950408889634
    for i in range(3):
        probs[i, 192:keys, :] = mm_nt(far[192:keys, i * 128:i * 128 + 128], bdq[i])
        v_far_t = far[:, 384 + i * 128:384 + i * 128 + 128].T
        for p in range(2):
            v_loc_t = local_rows(v_ref, i, p, 1).T
            for h in range(2):
                lanes = slice(p * 256 + h * 128, p * 256 + h * 128 + 128)
                scores = probs[i, :, lanes] * unit
                largest = jnp.max(scores, axis=0, keepdims=True)
                weights = jnp.exp2(scores - largest)
                weights = weights * (1.0 / jnp.sum(weights, axis=0, keepdims=True))
                probs[i, :, lanes] = weights
                low = weights.astype(BF)
                part = mm(v_far_t[h * 64:h * 64 + 64], low[:keys]) + mm(v_loc_t[h * 64:h * 64 + 64], low[keys:])
                attn_t[i * 128 + h * 64:i * 128 + h * 64 + 64, p * 128:p * 128 + 128] = part.astype(BF)

    wait_in(fg.at[1 - mp], mp_r.at[0])
    tall = 384 // (his // 2)
    for c in range(2):
        terms = mm(attn_t[...], fg[c]).astype(BF)
        for t in range(his // 2):
            gw_send[2 * t + c] = terms[t * tall:t * tall + tall]
    gw_land[hi] = gw_send[hi]
    for b in range(hi_bits):
        n = 1 << b
        each(n, hi, lambda j, b=b, n=n: far_copy(
            b, j, gw_send.at[sibling(hi // n) * n + j], gw_land.at[hi], r1g_s, r1g_r).start())
    attn = attn_t[...].T
    lo_send[...] = mm(attn, w_ref[:, pl.ds(pl.multiple_of((1 - mp) * 384, 128), 384)]).astype(BF)
    to_lo = pltpu.make_async_remote_copy(
        src_ref=lo_send, dst_ref=lo_land, send_sem=mp_s.at[1], recv_sem=mp_r.at[1],
        device_id=mp_id, device_id_type=MESH)
    to_lo.start()

    grad_attn = (mm_nt(fg[0], w_ref[:, 0:384]) + mm_nt(fg[1], w_ref[:, 384:768])).astype(BF)
    for i in range(3):
        for p in range(2):
            part = grad_attn[p * 128:p * 128 + 128, i * 128:i * 128 + 128]
            for h in range(2):
                at = p * 256 + h * 128
                bdo[i, at:at + 128, :] = part * masks[h]
        k_lanes = slice(i * 128, i * 128 + 128)
        v_lanes = slice(384 + i * 128, 384 + i * 128 + 128)
        gp_far = mm_nt(far[:, v_lanes], bdo[i])
        k_far_t = far[:, k_lanes].T
        d_scores, p_low = [], []
        for p in range(2):
            gp_loc = mm_nt(local_rows(v_ref, i, p, 1), bdo[i, p * 256:p * 256 + 256, :])
            k_loc_t = local_rows(k_ref, i, p, 0).T
            ds_half, pl_half = [], []
            for h in range(2):
                lanes = slice(p * 256 + h * 128, p * 256 + h * 128 + 128)
                weights = probs[i, :, lanes]
                grads = jnp.concatenate([gp_far[:, lanes], gp_loc[:, h * 128:h * 128 + 128]], axis=0)
                centre = jnp.sum(weights * grads, axis=0, keepdims=True)
                ds = (weights * (grads - centre) * HEAD ** -0.5).astype(BF)
                part = mm(k_far_t[h * 64:h * 64 + 64], ds[:keys]) + mm(k_loc_t[h * 64:h * 64 + 64], ds[keys:])
                dq_t[i * 128 + h * 64:i * 128 + h * 64 + 64, p * 128:p * 128 + 128] = part
                ds_half.append(ds)
                pl_half.append(weights.astype(BF))
            ds_p = jnp.concatenate(ds_half, axis=1)
            pl_p = jnp.concatenate(pl_half, axis=1)
            dk_l = mm(ds_p[keys:], bdq[i, p * 256:p * 256 + 256, :])
            dv_l = mm(pl_p[keys:], bdo[i, p * 256:p * 256 + 256, :])
            d_loc[p * 128:p * 128 + 128, k_lanes] = dk_l[0:128]
            d_loc[p * 128:p * 128 + 128, v_lanes] = dv_l[0:128]
            d_l1[64 * (1 - p):64 * (1 - p) + 64, k_lanes] = dk_l[128:192].astype(BF)
            d_l1[64 * (1 - p):64 * (1 - p) + 64, v_lanes] = dv_l[128:192].astype(BF)
            d_scores.append(ds_p[:keys])
            p_low.append(pl_p[:keys])
        dk_f = mm(jnp.concatenate(d_scores, axis=1), bdq[i])
        dv_f = mm(jnp.concatenate(p_low, axis=1), bdo[i])
        d_far[:, k_lanes] = dk_f[0:192]
        d_far[:, v_lanes] = dv_f[0:192]
        low_keys = min(keys, 384)
        d_send[:, k_lanes] = dk_f[192:low_keys].astype(BF)
        d_send[:, v_lanes] = dv_f[192:low_keys].astype(BF)
        if hi_bits > 3:
            d_f32[:, k_lanes] = dk_f[384:448]
            d_f32[:, v_lanes] = dv_f[384:448]

    for b in range(hi_bits):
        n, r = 1 << b, BLOCK >> b
        if b < 3:
            each(n, hi, lambda j, b=b, n=n, r=r: far_copy(
                b, j, d_send.at[pl.ds(pl.multiple_of(b * BLOCK + j * r, 16), r)],
                r1_land.at[pl.ds(pl.multiple_of(b * BLOCK + (hi % n) * r, 16), r)], r1_s, r1_r).start())
        else:
            each(n, hi, lambda j, b=b, n=n, r=r: far_copy(
                b, j, d_f32.at[pl.ds(pl.multiple_of(j * r, 8), r)],
                r1_f32.at[pl.ds(pl.multiple_of((hi % n) * r, 8), r)], r1_s, r1_r).start())

    for b in range(hi_bits):
        n = 1 << b
        each(n, hi, lambda j, n=n: wait_in(gw_land.at[sibling(hi // n) * n + j], r1g_r.at[n - 1 + j]))
    total = gw_land[0].astype(F32)
    for f in range(1, his):
        total = total + gw_land[f].astype(F32)
    gw_part[...] = total.astype(BF)
    gw_ar[lo] = gw_part[...]
    for b in range(NEAR_BITS):
        n = 1 << b
        each(n, lo, lambda j, b=b: near_copy(b, j, gw_part, gw_ar.at[lo], r2g_s, r2g_r).start())

    dq_out[...] = dq_t[...].T.astype(BF)

    for b in range(hi_bits):
        n, r = 1 << b, BLOCK >> b
        if b < 3:
            each(n, hi, lambda j, b=b, n=n, r=r: wait_in(
                r1_land.at[pl.ds(pl.multiple_of(b * BLOCK + j * r, 16), r)], r1_r.at[n - 1 + j]))
        else:
            each(n, hi, lambda j, b=b, n=n, r=r: wait_in(
                r1_f32.at[pl.ds(pl.multiple_of(j * r, 8), r)], r1_r.at[n - 1 + j]))
    cols = BLOCK * hi_bits
    landed = r1_land[...]
    if hi_bits > 3:
        landed = jnp.concatenate([landed, r1_f32[...].astype(BF)], axis=0)
    at_row, at_col = iota((64, cols), 0), iota((64, cols), 1)
    spread = jnp.zeros((64, cols), F32)
    for b in range(hi_bits):
        hit = (at_col // 64 == b) & (at_row // (1 << b) == at_col % (64 >> b))
        spread = jnp.where(hit, 0.5 ** b, spread)
    group_grad = mm(spread.astype(BF), landed).astype(BF)
    at_row, at_col = iota((192, 64), 0), iota((192, 64), 1)
    spread = jnp.zeros((192, 64), F32)
    for b in range(NEAR_BITS):
        base = sibling(lo // (1 << b)) * (1 << b)
        hit = (at_row // 64 == b) & (at_col == 8 * base + at_row % 64 // (8 >> b))
        spread = jnp.where(hit, 0.5 ** (3 - b), spread)
    msg[...] = (d_far[...] + mm(spread.astype(BF), group_grad)).astype(BF)

    for b in range(NEAR_BITS):
        n, r = 1 << b, BLOCK >> b
        each(n, lo, lambda j, b=b, n=n, r=r: near_copy(
            b, j, msg.at[pl.ds(pl.multiple_of(b * BLOCK + j * r, 16), r)],
            r2_land.at[pl.ds(pl.multiple_of(b * BLOCK + (lo % n) * r, 16), r)], r2_s, r2_r).start())

    for b in range(NEAR_BITS):
        n = 1 << b
        each(n, lo, lambda j, n=n: wait_in(gw_ar.at[sibling(lo // n) * n + j], r2g_r.at[n - 1 + j]))
    total = gw_ar[0].astype(F32)
    for e in range(1, NEAR):
        total = total + gw_ar[e].astype(F32)
    gw_part2 = total.astype(BF)
    gw_all[hi] = gw_part2
    for b in range(hi_bits):
        n = 1 << b
        each(n, hi, lambda j, b=b: far_copy(b, j, gw_all.at[hi], gw_all.at[hi], ag_s, ag_r).start())

    for b in range(NEAR_BITS):
        n, r = 1 << b, BLOCK >> b
        each(n, lo, lambda j, b=b, n=n, r=r: wait_in(
            r2_land.at[pl.ds(pl.multiple_of(b * BLOCK + j * r, 16), r)], r2_r.at[n - 1 + j]))
    terms = jnp.concatenate([r2_land[...], group_grad, d_l1[...]], axis=0)
    at_row, at_col = iota((256, 384), 0), iota((256, 384), 1)
    spread = jnp.zeros((256, 384), F32)
    for b in range(NEAR_BITS):
        hit = (at_col // 64 == b) & (at_row // (4 << b) == at_col % (64 >> b))
        spread = jnp.where(hit, 0.25 * 0.5 ** b, spread)
    spread = jnp.where((at_col // 64 == 3) & (at_col % 64 == 8 * lo + at_row // 32), 0.5 ** 5, spread)
    spread = jnp.where((at_col >= 256) & (at_col - 256 == at_row // 2), 0.5, spread)
    grads = d_loc[...] + mm(spread.astype(BF), terms)
    dk_out[...] = grads[:, 0:384].astype(BF)
    dv_out[...] = grads[:, 384:768].astype(BF)

    mine = mm(attn, w_ref[:, pl.ds(pl.multiple_of(mp * 384, 128), 384)])
    wait_in(lo_land, mp_r.at[1])
    lo_out[...] = (mine + lo_land[...].astype(F32)).astype(BF)

    for b in range(hi_bits):
        n = 1 << b
        each(n, hi, lambda j, n=n: wait_in(gw_all.at[sibling(hi // n) * n + j], ag_r.at[n - 1 + j]))
    for f in range(his):
        gw_out[f // 2 * tall:f // 2 * tall + tall, f % 2 * 384:f % 2 * 384 + 384] = gw_all[f].astype(F32)

    for b in range(NEAR_BITS):
        n, r = 1 << b, BLOCK >> b

        def near_done(j, b=b, n=n, r=r):
            wait_in(near_rows.at[pl.ds(112, 16)], f1u_s.at[n - 1 + j])
            wait_in(near_rows.at[pl.ds(near_at[b], r)], f1_s.at[n - 1 + j])
            wait_in(msg.at[pl.ds(pl.multiple_of(b * BLOCK + j * r, 16), r)], r2_s.at[n - 1 + j])
            wait_in(gw_part, r2g_s.at[n - 1 + j])

        each(n, lo, near_done)
    for b in range(hi_bits):
        n, r = 1 << b, BLOCK >> b

        def far_done(j, b=b, n=n, r=r):
            if b < 3:
                wait_in(up.at[pl.ds(up_at[b], r)], f2_s.at[n - 1 + j])
                wait_in(d_send.at[pl.ds(pl.multiple_of(b * BLOCK + j * r, 16), r)], r1_s.at[n - 1 + j])
            else:
                wait_in(up_f32, f2_s.at[n - 1 + j])
                wait_in(d_f32.at[pl.ds(pl.multiple_of(j * r, 8), r)], r1_s.at[n - 1 + j])
            wait_in(gw_send.at[sibling(hi // n) * n + j], r1g_s.at[n - 1 + j])
            wait_in(gw_all.at[hi], ag_s.at[n - 1 + j])

        each(n, hi, far_done)
    to_mp.wait_send()
    to_lo.wait_send()


def on_device(query_rows, key_rows, value_rows, w_output, grad_output):
    hi_bits = (lax.axis_size("ctx") // NEAR).bit_length() - 1
    his = 1 << hi_bits
    keys = (NEAR_BITS + hi_bits) * BLOCK
    low_rows = 64 * min(hi_bits, 3)
    tall = 384 // (his // 2)
    vm = pltpu.VMEM
    dma = pltpu.SemaphoreType.DMA
    near_sem, far_sem = dma((NEAR - 1,)), dma((his - 1,))
    scratch = [
        vm((128, 768), BF),
        vm((128, 768), BF),
        vm((keys, 768), BF),
        vm((64, 768), F32),
        vm((NEAR, 16, 768), BF),
        vm((112, 768), BF),
        vm((8, 768), F32),
        vm((2, 256, 384), BF),
        vm((3, 512, 128), BF),
        vm((3, 512, 128), BF),
        vm((3, keys + 192, 512), F32),
        vm((384, 256), BF),
        vm((384, 256), F32),
        vm((192, 768), F32),
        vm((low_rows, 768), BF),
        vm((64, 768), F32),
        vm((low_rows, 768), BF),
        vm((64, 768), F32),
        vm((192, 768), BF),
        vm((192, 768), BF),
        vm((256, 768), F32),
        vm((128, 768), BF),
        vm((his, tall, 384), BF),
        vm((his, tall, 384), BF),
        vm((tall, 384), BF),
        vm((NEAR, tall, 384), BF),
        vm((his, tall, 384), BF),
        vm((256, 384), BF),
        vm((256, 384), BF),
        near_sem, near_sem, near_sem, near_sem,
        far_sem, far_sem, far_sem, far_sem, far_sem, far_sem,
        near_sem, near_sem, near_sem, near_sem,
        far_sem, far_sem,
        dma((2,)), dma((2,)),
    ]
    rows = jax.ShapeDtypeStruct((256, 384), BF)
    whole = pl.BlockSpec(memory_space=pltpu.VMEM)
    return pl.pallas_call(
        functools.partial(kernel, hi_bits),
        out_shape=(rows, rows, rows, rows, jax.ShapeDtypeStruct((384, 768), F32)),
        in_specs=[whole] * 5,
        out_specs=(whole,) * 5,
        scratch_shapes=scratch,
        compiler_params=pltpu.CompilerParams(
            collective_id=0, has_side_effects=True, vmem_limit_bytes=48 * 1024 * 1024),
        cost_estimate=pl.CostEstimate(flops=1_200_000_000, bytes_accessed=4_000_000, transcendentals=1_000_000),
    )(query_rows, key_rows, value_rows, w_output, grad_output)


def solution(mesh):
    placed = (P("ctx", "mp"), P("ctx", "mp"), P("ctx", "mp"), P("mp", None), P("ctx", "mp"))
    return jax.shard_map(
        on_device,
        mesh=mesh,
        in_specs=placed,
        out_specs=(P("ctx", "mp"), P("ctx", "mp"), P("ctx", "mp"), P("ctx", "mp"), P("mp", None)),
        check_vma=False,
    )
```

```python
import jax
import jax.numpy as jnp
from jax import lax
from jax.experimental import pallas as pl
from jax.experimental.pallas import tpu as pltpu
from jax.sharding import PartitionSpec as P

HEAD = 64
BLOCK = 64
NEAR = 8
NEAR_BITS = 3
FAR = 16
FAR_BITS = 4
KEYS = (NEAR_BITS + FAR_BITS) * BLOCK
CHUNK = 24
MESH = pl.DeviceIdType.MESH
BF = jnp.bfloat16
F32 = jnp.float32


def iota(shape, axis):
    return lax.broadcasted_iota(jnp.int32, shape, axis)


def where_one(condition, weight):
    return jnp.where(condition, weight, 0.0).astype(BF)


def mm(a, b):
    return jnp.dot(a, b, preferred_element_type=F32)


def mm_nt(a, b):
    return lax.dot_general(a, b, (((1,), (1,)), ((), ())), preferred_element_type=F32)


def pool(rows):
    count = rows.shape[0]
    out = max(count // 2, 16)
    halves = where_one(iota((out, count), 1) // 2 == iota((out, count), 0), 0.5)
    return mm(halves, rows).astype(BF)


def sibling(index):
    return index + 1 - 2 * (index % 2)


def kernel(
    q_hbm, k_hbm, v_hbm, w_hbm, go_hbm,
    lo_hbm, dq_hbm, dk_hbm, dv_hbm, gw_hbm,
    lo_out, dq_out, dk_out, dv_out,
    q_ref, k_ref, v_ref, w_ref, go_ref,
    near_rows, level1, far, far_f32, ug, up, up_f32, fg, bdq, bdo, probs, attn_t, dq_t,
    d_far, d_x, d_land, d_near, d_send, d_f32, r1_land, r1_f32, gg, msg0, msg, r2_land, d_loc, d_l1,
    gw_x, gw_pl, gw_own, gw_send, gw_land, gw_part, gw_ar, gw_all, lo_send, lo_land,
    ld, st, f1_s, f1_r, f2_s, f2_r, r1_s, r1_r, r2_s, r2_r, gw_s, gw_r, pair_s, pair_r, mp_s, mp_r,
):
    place = lax.axis_index("ctx")
    mp = lax.axis_index("mp")
    hi = place // NEAR
    lo = place % NEAR
    core = lo % 2
    depth = lo // 2

    def near_id(e):
        return (hi * NEAR + e, mp)

    def far_id(f):
        return (f * NEAR + lo, mp)

    mp_id = (place, 1 - mp)

    def send(src, dst, s, r, to):
        pltpu.make_async_remote_copy(
            src_ref=src, dst_ref=dst, send_sem=s, recv_sem=r, device_id=to, device_id_type=MESH).start()

    def near_peer(b, j):
        return sibling(lo // (1 << b)) * (1 << b) + j

    def far_peer(b, j):
        return sibling(hi // (1 << b)) * (1 << b) + j

    def each(n, mine, body):
        if n <= 2:
            for j in range(n):
                body((j + mine) % n)
        else:
            def step(t, c):
                body((t + mine) % n)
                return c
            lax.fori_loop(0, n, step, 0)

    def landed_in(ref, sem):
        pltpu.make_async_copy(ref, ref, sem).wait()

    loads = [pltpu.make_async_copy(src, dst, ld.at[n]) for n, (src, dst) in enumerate(
        ((k_hbm, k_ref), (v_hbm, v_ref), (go_hbm, go_ref), (q_hbm, q_ref), (w_hbm, w_ref)))]
    for load in loads:
        load.start()
    stores = [pltpu.make_async_copy(src, dst, st.at[n]) for n, (src, dst) in enumerate(
        ((lo_out, lo_hbm), (dq_out, dq_hbm), (dk_out, dk_hbm), (dv_out, dv_hbm), (gw_all, gw_hbm)))]
    barrier = pltpu.get_barrier_semaphore()
    for b in range(NEAR_BITS):
        each(1 << b, lo, lambda j, b=b: pl.semaphore_signal(
            barrier, inc=1, device_id=near_id(near_peer(b, j)), device_id_type=MESH))
    for b in range(FAR_BITS):
        each(1 << b, hi, lambda j, b=b: pl.semaphore_signal(
            barrier, inc=1, device_id=far_id(far_peer(b, j)), device_id_type=MESH))
    pl.semaphore_signal(barrier, inc=1, device_id=mp_id, device_id_type=MESH)

    loads[0].wait()
    loads[1].wait()
    rows = jnp.concatenate([k_ref[...], v_ref[...]], axis=1)

    def keep(ref, start, rows):
        for side in range(2):
            ref[side, start:start + rows.shape[0], :] = rows[:, side * 384:side * 384 + 384]

    rows = pool(rows)
    keep(level1, 0, rows)
    rows = pool(rows)
    keep(near_rows, 0, rows)
    rows = pool(rows)
    keep(near_rows, 64, rows)
    rows = pool(rows)
    keep(near_rows, 96, rows)
    first = pool(rows)
    step_up = where_one(iota((16, 16), 1) // 2 + 8 == iota((16, 16), 0), 0.5)
    upper = first
    for _ in range(3):
        upper = (first.astype(F32) + mm(step_up, upper)).astype(BF)
    keep(near_rows, 112, upper)
    ug[lo] = near_rows[core, 112:128, :]

    pl.semaphore_wait(barrier, NEAR - 1 + FAR - 1 + 1)

    for b in range(NEAR_BITS):
        each(1 << b, lo, lambda j, b=b: send(
            near_rows.at[near_peer(b, j) % 2, pl.ds(112, 16)], ug.at[lo], f1_s.at[0], f1_r.at[0],
            near_id(near_peer(b, j))))
    each(2, lo, lambda j: send(
        near_rows.at[j, pl.ds(64, 32)],
        far.at[j, pl.ds(pl.multiple_of(64 + core * 32, 16), 32)], f1_s.at[1], f1_r.at[1], near_id(near_peer(1, j))))
    each(4, lo, lambda j: send(
        near_rows.at[j % 2, pl.ds(96, 16)],
        far.at[j % 2, pl.ds(pl.multiple_of(128 + lo % 4 * 16, 16), 16)], f1_s.at[1], f1_r.at[1],
        near_id(near_peer(2, j))))
    partner = near_id(sibling(lo))
    send(near_rows.at[:, pl.ds(0, 64)], far.at[:, pl.ds(0, 64)], pair_s.at[0], pair_r.at[0], partner)

    lane_low = iota((128, 128), 1) < HEAD
    masks = (where_one(lane_low, 1.0), where_one(jnp.logical_not(lane_low), 1.0))

    def local_rows(own, i, p, side):
        lanes = slice(i * 128, i * 128 + 128)
        return jnp.concatenate(
            [own[p * 128:p * 128 + 128, lanes], level1[side, 64 * (1 - p):64 * (1 - p) + 64, lanes]], axis=0)

    loads[3].wait()
    loads[4].wait()
    for i in range(3):
        for p in range(2):
            part = q_ref[p * 128:p * 128 + 128, i * 128:i * 128 + 128]
            for h in range(2):
                at = p * 256 + h * 128
                bdq[i, at:at + 128, :] = part * masks[h]
        for p in range(2):
            probs[i, KEYS:KEYS + 192, p * 256:p * 256 + 256] = mm_nt(
                local_rows(k_ref, i, p, 0), bdq[i, p * 256:p * 256 + 256, :])

    landed_in(ug.at[pl.ds(0, NEAR - 1)], f1_r.at[0])
    gathered = ug[...].reshape(NEAR * 16, 384)
    a = iota((128, 128), 0)
    source = jnp.where(
        a < 64, a // 8 * 16 + a % 8,
        jnp.where(a < 96, (a - 64) // 4 * 16 + 8 + a % 4,
                  jnp.where(a < 112, (a - 96) // 2 * 16 + 12 + a % 2, (a - 112) * 16 + 14)))
    levels = mm(where_one(iota((128, 128), 1) == source, 1.0), gathered)
    up[...] = levels[0:112].astype(BF)
    up_f32[...] = levels[112:120]

    each(8, hi, lambda j: send(
        up_f32, far_f32.at[pl.ds(pl.multiple_of(hi % 8 * 8, 8), 8)], f2_s.at[1], f2_r.at[1], far_id(far_peer(3, j))))
    for b in reversed(range(3)):
        r = BLOCK >> b
        each(1 << b, hi, lambda j, b=b, r=r: send(
            up.at[pl.ds((0, 64, 96)[b], r)],
            far.at[core, pl.ds(pl.multiple_of((3 + b) * BLOCK + hi % (1 << b) * r, 16), r)],
            f2_s.at[0], f2_r.at[0], far_id(far_peer(b, j))))

    loads[2].wait()
    to_mp = pltpu.make_async_remote_copy(
        src_ref=go_ref, dst_ref=fg.at[mp], send_sem=mp_s.at[0], recv_sem=mp_r.at[0],
        device_id=mp_id, device_id_type=MESH)
    to_mp.start()
    fg[mp] = go_ref[...]

    landed_in(far.at[core, pl.ds(64, 128)], f1_r.at[1])
    send(far.at[core, pl.ds(64, 128)], far.at[core, pl.ds(64, 128)], pair_s.at[1], pair_r.at[1], partner)
    landed_in(far.at[:, pl.ds(0, 64)], pair_r.at[0])
    landed_in(far.at[1 - core, pl.ds(64, 128)], pair_r.at[1])
    for i in range(3):
        probs[i, 0:192, :] = mm_nt(far[0, 0:192, i * 128:i * 128 + 128], bdq[i])

    landed_in(far_f32, f2_r.at[1])
    far[core, 384:448, :] = far_f32[...].astype(BF)
    landed_in(far.at[core, pl.ds(192, 192)], f2_r.at[0])
    send(far.at[core, pl.ds(192, 256)], far.at[core, pl.ds(192, 256)], pair_s.at[2], pair_r.at[2], partner)
    landed_in(far.at[1 - core, pl.ds(192, 256)], pair_r.at[2])

    unit = HEAD ** -0.5 * 1.4426950408889634
    for i in range(3):
        probs[i, 192:KEYS, :] = mm_nt(far[0, 192:KEYS, i * 128:i * 128 + 128], bdq[i])
        v_far_t = far[1, :, i * 128:i * 128 + 128].T
        for p in range(2):
            v_loc_t = local_rows(v_ref, i, p, 1).T
            for h in range(2):
                lanes = slice(p * 256 + h * 128, p * 256 + h * 128 + 128)
                scores = probs[i, :, lanes] * unit
                largest = jnp.max(scores, axis=0, keepdims=True)
                weights = jnp.exp2(scores - largest)
                weights = weights * (1.0 / jnp.sum(weights, axis=0, keepdims=True))
                probs[i, :, lanes] = weights
                low = weights.astype(BF)
                part = mm(v_far_t[h * 64:h * 64 + 64], low[:KEYS]) + mm(v_loc_t[h * 64:h * 64 + 64], low[KEYS:])
                attn_t[i * 128 + h * 64:i * 128 + h * 64 + 64, p * 128:p * 128 + 128] = part.astype(BF)

    def chunk_of(terms, f):
        pieces = [terms[CHUNK * f:CHUNK * f + CHUNK, c * 128:c * 128 + 128] for c in range(3)]
        return jnp.concatenate(pieces + [jnp.zeros((8, 128), F32)], axis=0)

    landed_in(fg.at[1 - mp], mp_r.at[0])
    terms = mm(attn_t[...], fg[1 - core])
    for f in range(FAR):
        gw_x[f] = chunk_of(terms, f).astype(BF)
    send(gw_x, gw_pl, pair_s.at[3], pair_r.at[3], partner)

    attn = attn_t[...].T
    lo_send[...] = mm(attn, w_ref[:, pl.ds(pl.multiple_of((1 - mp) * 384, 128), 384)]).astype(BF)
    to_lo = pltpu.make_async_remote_copy(
        src_ref=lo_send, dst_ref=lo_land, send_sem=mp_s.at[1], recv_sem=mp_r.at[1],
        device_id=mp_id, device_id_type=MESH)
    to_lo.start()
    terms = mm(attn_t[...], fg[core])
    for f in range(FAR):
        gw_own[f] = chunk_of(terms, f)
    landed_in(gw_pl, pair_r.at[3])
    gw_send[...] = (gw_own[...] + gw_pl[...].astype(F32)).astype(BF)
    gw_land[hi] = gw_send[hi]
    for b in range(FAR_BITS):
        each(1 << b, hi, lambda j, b=b: send(
            gw_send.at[far_peer(b, j)], gw_land.at[hi], gw_s.at[0], gw_r.at[0], far_id(far_peer(b, j))))

    grad_attn = (mm_nt(fg[0], w_ref[:, 0:384]) + mm_nt(fg[1], w_ref[:, 384:768])).astype(BF)
    for i in range(3):
        lanes_i = slice(i * 128, i * 128 + 128)
        for p in range(2):
            part = grad_attn[p * 128:p * 128 + 128, lanes_i]
            for h in range(2):
                at = p * 256 + h * 128
                bdo[i, at:at + 128, :] = part * masks[h]
        gp_far = mm_nt(far[1, :, lanes_i], bdo[i])
        k_far_t = far[0, :, lanes_i].T
        d_scores, p_low = [], []
        for p in range(2):
            gp_loc = mm_nt(local_rows(v_ref, i, p, 1), bdo[i, p * 256:p * 256 + 256, :])
            k_loc_t = local_rows(k_ref, i, p, 0).T
            ds_half, pl_half = [], []
            for h in range(2):
                lanes = slice(p * 256 + h * 128, p * 256 + h * 128 + 128)
                weights = probs[i, :, lanes]
                grads = jnp.concatenate([gp_far[:, lanes], gp_loc[:, h * 128:h * 128 + 128]], axis=0)
                centre = jnp.sum(weights * grads, axis=0, keepdims=True)
                ds = (weights * (grads - centre) * HEAD ** -0.5).astype(BF)
                part = mm(k_far_t[h * 64:h * 64 + 64], ds[:KEYS]) + mm(k_loc_t[h * 64:h * 64 + 64], ds[KEYS:])
                dq_t[i * 128 + h * 64:i * 128 + h * 64 + 64, p * 128:p * 128 + 128] = part
                ds_half.append(ds)
                pl_half.append(weights.astype(BF))
            ds_p = jnp.concatenate(ds_half, axis=1)
            pl_p = jnp.concatenate(pl_half, axis=1)
            d_scores.append(ds_p)
            p_low.append(pl_p)
        for side, left, right in ((0, d_scores, bdq), (1, p_low, bdo)):
            grads = mm(jnp.concatenate([part[:KEYS] for part in left], axis=1), right[i])
            d_far[side, :, lanes_i] = grads
            d_x[side, :, lanes_i] = grads[64:KEYS].astype(BF)
            for p in range(2):
                grads = mm(left[p][KEYS:], right[i, p * 256:p * 256 + 256, :])
                d_loc[side, p * 128:p * 128 + 128, lanes_i] = grads[0:128]
                d_l1[side, 64 * (1 - p):64 * (1 - p) + 64, lanes_i] = grads[128:192].astype(BF)

    send(d_x.at[1 - core], d_land, pair_s.at[4], pair_r.at[4], partner)

    landed_in(d_land, pair_r.at[4])
    total = d_far[core, 64:KEYS, :] + d_land[...].astype(F32)
    d_send[...] = total[128:320].astype(BF)
    d_f32[...] = total[320:384]
    d_near[...] = total[0:128]
    each(8, hi, lambda j: send(
        d_f32.at[pl.ds(pl.multiple_of(j * 8, 8), 8)], r1_f32.at[pl.ds(pl.multiple_of(hi % 8 * 8, 8), 8)],
        r1_s.at[1], r1_r.at[1], far_id(far_peer(3, j))))
    for b in reversed(range(3)):
        r = BLOCK >> b
        each(1 << b, hi, lambda j, b=b, r=r: send(
            d_send.at[pl.ds(pl.multiple_of(b * BLOCK + j * r, 16), r)],
            r1_land.at[pl.ds(pl.multiple_of(b * BLOCK + hi % (1 << b) * r, 16), r)],
            r1_s.at[0], r1_r.at[0], far_id(far_peer(b, j))))

    landed_in(gw_land.at[pl.ds(0, FAR - 1)], gw_r.at[0])
    total = gw_land[0].astype(F32)
    for f in range(1, FAR):
        total = total + gw_land[f].astype(F32)
    gw_part[...] = total.astype(BF)
    gw_ar[depth] = gw_part[...]
    for t in range(1, 4):
        other = (depth + t) % 4
        send(gw_part, gw_ar.at[depth], gw_s.at[1], gw_r.at[1], near_id(other * 2 + core))

    landed_in(gw_ar.at[pl.ds(0, 3)], gw_r.at[1])
    total = gw_ar[0].astype(F32)
    for e in range(1, 4):
        total = total + gw_ar[e].astype(F32)
    gw_all[core, hi] = total.astype(BF)
    for b in range(FAR_BITS):
        each(1 << b, hi, lambda j, b=b: send(
            gw_all.at[core, hi], gw_all.at[core, hi], gw_s.at[2], gw_r.at[2 + b // 3], far_id(far_peer(b, j))))

    dq_out[...] = dq_t[...].T.astype(BF)
    stores[1].start()
    mine = mm(attn, w_ref[:, pl.ds(pl.multiple_of(mp * 384, 128), 384)])

    landed_in(r1_land, r1_r.at[0])
    landed_in(r1_f32, r1_r.at[1])
    landed = jnp.concatenate([r1_land[...], r1_f32[...].astype(BF)], axis=0)
    at_row, at_col = iota((64, 256), 0), iota((64, 256), 1)
    spread = jnp.zeros((64, 256), F32)
    for b in range(FAR_BITS):
        hit = (at_col // 64 == b) & (at_row // (1 << b) == at_col % (64 >> b))
        spread = jnp.where(hit, 0.5 ** b, spread)
    group_grad = mm(spread.astype(BF), landed).astype(BF)
    gg[core] = group_grad
    gg[1 - core] = jnp.zeros((64, 384), BF)
    at_row, at_col = iota((192, 64), 0), iota((192, 64), 1)
    spread = jnp.zeros((192, 64), F32)
    for b in range(NEAR_BITS):
        base = sibling(lo // (1 << b)) * (1 << b)
        hit = (at_row // 64 == b) & (at_col == 8 * base + at_row % 64 // (8 >> b))
        spread = jnp.where(hit, 0.5 ** (3 - b), spread)
    spread = mm(spread.astype(BF), group_grad)
    msg[...] = (d_near[...] + spread[64:192]).astype(BF)
    msg0[core] = (d_far[core, 0:64, :] + spread[0:64]).astype(BF)
    msg0[1 - core] = d_far[1 - core, 0:64, :].astype(BF)

    each(2, lo, lambda j: send(
        msg.at[pl.ds(pl.multiple_of(j * 32, 16), 32)], r2_land.at[core, pl.ds(64, 32)],
        r2_s.at[0], r2_r.at[0], near_id(near_peer(1, j))))
    each(4, lo, lambda j: send(
        msg.at[pl.ds(pl.multiple_of(64 + j * 16, 16), 16)],
        r2_land.at[core, pl.ds(pl.multiple_of(96 + depth % 2 * 16, 16), 16)],
        r2_s.at[0], r2_r.at[0], near_id(near_peer(2, j))))
    send(msg0, r2_land.at[:, pl.ds(0, 64)], pair_s.at[5], pair_r.at[5], partner)

    landed_in(gw_all.at[core, pl.ds(0, 7)], gw_r.at[2])
    eight = pl.multiple_of(hi // 8 * 8, 8)
    send(gw_all.at[core, pl.ds(eight, 8)], gw_all.at[core, pl.ds(eight, 8)], pair_s.at[6], pair_r.at[6], partner)
    landed_in(gw_all.at[core, pl.ds(0, 8)], gw_r.at[3])
    eight = pl.multiple_of(sibling(hi // 8) * 8, 8)
    send(gw_all.at[core, pl.ds(eight, 8)], gw_all.at[core, pl.ds(eight, 8)], pair_s.at[7], pair_r.at[7], partner)

    landed_in(r2_land.at[:, pl.ds(64, 64)], r2_r.at[0])
    landed_in(r2_land.at[:, pl.ds(0, 64)], pair_r.at[5])
    at_row, at_col = iota((256, 320), 0), iota((256, 320), 1)
    hits = (
        (at_col < 64) & (at_row // 4 == at_col),
        (at_col >= 64) & (at_col < 96) & (at_row // 8 == at_col - 64),
        (at_col >= 96) & (at_col < 128) & (at_row // 16 == at_col % 16),
        (at_col >= 128) & (at_col < 192) & (8 * lo + at_row // 32 == at_col - 128),
        (at_col >= 192) & (at_row // 2 == at_col - 192),
    )
    spread = jnp.zeros((256, 320), F32)
    for hit, weight in zip(hits, (0.25, 0.125, 0.0625, 0.03125, 0.5)):
        spread = jnp.where(hit, weight, spread)
    spread = spread.astype(BF)
    for side, out in ((0, dk_out), (1, dv_out)):
        terms = jnp.concatenate([r2_land[side], gg[side], d_l1[side]], axis=0)
        out[...] = (d_loc[side] + mm(spread, terms)).astype(BF)
        stores[2 + side].start()

    landed_in(lo_land, mp_r.at[1])
    lo_out[...] = (mine + lo_land[...].astype(F32)).astype(BF)
    stores[0].start()

    landed_in(gw_all.at[1 - core, pl.ds(0, 8)], pair_r.at[6])
    landed_in(gw_all.at[1 - core, pl.ds(0, 8)], pair_r.at[7])
    stores[4].start()

    landed_in(ug.at[pl.ds(0, NEAR - 1)], f1_s.at[0])
    landed_in(far.at[core, pl.ds(64, 128)], f1_s.at[1])
    landed_in(far.at[core, pl.ds(192, 192)], f2_s.at[0])
    landed_in(far_f32, f2_s.at[1])
    landed_in(r1_land, r1_s.at[0])
    landed_in(r1_f32, r1_s.at[1])
    landed_in(msg, r2_s.at[0])
    landed_in(gw_land.at[pl.ds(0, FAR - 1)], gw_s.at[0])
    landed_in(gw_ar.at[pl.ds(0, 3)], gw_s.at[1])
    landed_in(gw_land.at[pl.ds(0, FAR - 1)], gw_s.at[2])
    landed_in(msg0, pair_s.at[0])
    landed_in(msg, pair_s.at[1])
    landed_in(far.at[core, pl.ds(192, 256)], pair_s.at[2])
    landed_in(gw_x, pair_s.at[3])
    landed_in(d_land, pair_s.at[4])
    landed_in(msg0, pair_s.at[5])
    landed_in(gw_all.at[core, pl.ds(0, 8)], pair_s.at[6])
    landed_in(gw_all.at[core, pl.ds(0, 8)], pair_s.at[7])
    to_mp.wait_send()
    to_lo.wait_send()
    for store in stores:
        store.wait()


def hand_over(*refs):
    given, out, held, whole, sem = refs[0:5], refs[5:10], refs[10:15], refs[15], refs[16]
    first = [pltpu.make_async_copy(given[n], held[n], sem.at[n]) for n in range(5)]
    second = [pltpu.make_async_copy(held[n], out[n], sem.at[5 + n]) for n in range(4)]
    second.append(pltpu.make_async_copy(whole, out[4], sem.at[9]))
    for n in (4, 0, 1, 2, 3):
        first[n].start()
    first[4].wait()
    for side in range(2):
        for f in range(FAR):
            part = held[4][side, f].astype(F32)
            for c in range(3):
                at = side * 384 + c * 128
                whole[CHUNK * f:CHUNK * f + CHUNK, at:at + 128] = part[c * CHUNK:c * CHUNK + CHUNK]
    second[4].start()
    for n in range(4):
        first[n].wait()
        second[n].start()
    for copy in second:
        copy.wait()


def on_device(query_rows, key_rows, value_rows, w_output, grad_output):
    vm = pltpu.VMEM
    dma = pltpu.SemaphoreType.DMA
    piece = (80, 128)
    scratch = [
        vm((256, 384), BF), vm((256, 384), BF), vm((256, 384), BF), vm((256, 384), BF),
        vm((256, 384), BF), vm((256, 384), BF), vm((256, 384), BF), vm((384, 768), BF), vm((256, 384), BF),
        vm((2, 128, 384), BF),
        vm((2, 128, 384), BF),
        vm((2, KEYS, 384), BF),
        vm((64, 384), F32),
        vm((NEAR, 16, 384), BF),
        vm((112, 384), BF),
        vm((8, 384), F32),
        vm((2, 256, 384), BF),
        vm((3, 512, 128), BF),
        vm((3, 512, 128), BF),
        vm((3, KEYS + 192, 512), F32),
        vm((384, 256), BF),
        vm((384, 256), F32),
        vm((2, KEYS, 384), F32),
        vm((2, 384, 384), BF),
        vm((384, 384), BF),
        vm((128, 384), F32),
        vm((192, 384), BF),
        vm((64, 384), F32),
        vm((192, 384), BF),
        vm((64, 384), F32),
        vm((2, 64, 384), BF),
        vm((2, 64, 384), BF),
        vm((128, 384), BF),
        vm((2, 128, 384), BF),
        vm((2, 256, 384), F32),
        vm((2, 128, 384), BF),
        vm((FAR,) + piece, BF),
        vm((FAR,) + piece, BF),
        vm((FAR,) + piece, F32),
        vm((FAR,) + piece, BF),
        vm((FAR,) + piece, BF),
        vm(piece, BF),
        vm((4,) + piece, BF),
        vm((2, FAR) + piece, BF),
        vm((256, 384), BF),
        vm((256, 384), BF),
        dma((5,)),
        dma((5,)),
        dma((2,)), dma((2,)),
        dma((2,)), dma((2,)),
        dma((2,)), dma((2,)),
        dma((1,)), dma((1,)),
        dma((3,)), dma((4,)),
        dma((8,)), dma((8,)),
        dma((2,)), dma((2,)),
    ]
    rows = jax.ShapeDtypeStruct((256, 384), BF)
    chunks = jax.ShapeDtypeStruct((2, FAR) + piece, BF)
    in_hbm = pl.BlockSpec(memory_space=pltpu.HBM)
    results = pl.pallas_call(
        kernel,
        out_shape=(rows, rows, rows, rows, chunks),
        in_specs=[in_hbm] * 5,
        out_specs=(in_hbm,) * 5,
        scratch_shapes=scratch,
        compiler_params=pltpu.CompilerParams(
            collective_id=0, has_side_effects=True, vmem_limit_bytes=58 * 1024 * 1024),
        cost_estimate=pl.CostEstimate(flops=1_200_000_000, bytes_accessed=4_000_000, transcendentals=1_000_000),
    )(query_rows, key_rows, value_rows, w_output, grad_output)
    held = [vm((256, 384), BF)] * 4 + [vm((2, FAR) + piece, BF), vm((384, 768), F32)]
    return pl.pallas_call(
        hand_over,
        out_shape=(rows, rows, rows, rows, jax.ShapeDtypeStruct((384, 768), F32)),
        in_specs=[in_hbm] * 5,
        out_specs=(in_hbm,) * 5,
        scratch_shapes=held + [dma((10,))],
        compiler_params=pltpu.CompilerParams(vmem_limit_bytes=58 * 1024 * 1024),
    )(*results)


def solution(mesh):
    placed = (P("ctx", "mp"), P("ctx", "mp"), P("ctx", "mp"), P("mp", None), P("ctx", "mp"))
    return jax.shard_map(
        on_device,
        mesh=mesh,
        in_specs=placed,
        out_specs=(P("ctx", "mp"), P("ctx", "mp"), P("ctx", "mp"), P("ctx", "mp"), P("mp", None)),
        check_vma=False,
    )
```

```python
import jax
import jax.numpy as jnp
from jax import lax
from jax.experimental import pallas as pl
from jax.experimental.pallas import tpu as pltpu
from jax.sharding import PartitionSpec as P

HEAD = 64
BLOCK = 64
NEAR = 8
NEAR_BITS = 3
FAR = 16
FAR_BITS = 4
KEYS = (NEAR_BITS + FAR_BITS) * BLOCK
CHUNK = 24
MESH = pl.DeviceIdType.MESH
BF = jnp.bfloat16
F32 = jnp.float32


def iota(shape, axis):
    return lax.broadcasted_iota(jnp.int32, shape, axis)


def where_one(condition, weight):
    return jnp.where(condition, weight, 0.0).astype(BF)


def mm(a, b):
    return jnp.dot(a, b, preferred_element_type=F32)


def mm_nt(a, b):
    return lax.dot_general(a, b, (((1,), (1,)), ((), ())), preferred_element_type=F32)


def sibling(index):
    return index + 1 - 2 * (index % 2)


def kernel(
    q_hbm, k_hbm, v_hbm, w_hbm, go_hbm,
    lo_hbm, dq_hbm, dk_hbm, dv_hbm, gw_hbm,
    lo_out, dq_out, dk_out, dv_out,
    q_ref, k_ref, v_ref, w_ref, go_ref,
    steps_ref, upper_ref, to_group, to_near, to_rows, k_loc_t, v_loc_t, near_rows, level1, far, far_f32, ug, up, up_f32, fg, bdq, bdo, probs, attn_t, dq_t,
    d_far, d_x, d_land, d_near, d_send, d_f32, r1_land, r1_f32, gg, msg0, msg, r2_land, d_loc, d_l1,
    gw_x, gw_pl, gw_own, gw_send, gw_land, gw_part, gw_ar, gw_all, lo_send, lo_land,
    ld, st, f1_s, f1_r, f2_s, f2_r, r1_s, r1_r, r2_s, r2_r, gw_s, gw_r, pair_s, pair_r, mp_s, mp_r,
):
    place = lax.axis_index("ctx")
    mp = lax.axis_index("mp")
    hi = place // NEAR
    lo = place % NEAR
    core = lo % 2
    depth = lo // 2

    def near_id(e):
        return (hi * NEAR + e, mp)

    def far_id(f):
        return (f * NEAR + lo, mp)

    mp_id = (place, 1 - mp)

    def send(src, dst, s, r, to):
        pltpu.make_async_remote_copy(
            src_ref=src, dst_ref=dst, send_sem=s, recv_sem=r, device_id=to, device_id_type=MESH).start()

    def near_peer(b, j):
        return sibling(lo // (1 << b)) * (1 << b) + j

    def far_peer(b, j):
        return sibling(hi // (1 << b)) * (1 << b) + j

    def each(n, mine, body):
        if n <= 2:
            for j in range(n):
                body((j + mine) % n)
        else:
            def step(t, c):
                body((t + mine) % n)
                return c
            lax.fori_loop(0, n, step, 0)

    def landed_in(ref, sem):
        pltpu.make_async_copy(ref, ref, sem).wait()

    loads = [pltpu.make_async_copy(src, dst, ld.at[n]) for n, (src, dst) in enumerate(
        ((k_hbm, k_ref), (v_hbm, v_ref), (go_hbm, go_ref), (q_hbm, q_ref), (w_hbm, w_ref)))]
    for load in loads:
        load.start()
    stores = [pltpu.make_async_copy(src, dst, st.at[n]) for n, (src, dst) in enumerate(
        ((lo_out, lo_hbm), (dq_out, dq_hbm), (dk_out, dk_hbm), (dv_out, dv_hbm), (gw_all, gw_hbm)))]
    barrier = pltpu.get_barrier_semaphore()
    for b in range(NEAR_BITS):
        each(1 << b, lo, lambda j, b=b: pl.semaphore_signal(
            barrier, inc=1, device_id=near_id(near_peer(b, j)), device_id_type=MESH))
    for b in range(FAR_BITS):
        each(1 << b, hi, lambda j, b=b: pl.semaphore_signal(
            barrier, inc=1, device_id=far_id(far_peer(b, j)), device_id_type=MESH))
    pl.semaphore_signal(barrier, inc=1, device_id=mp_id, device_id_type=MESH)

    loads[0].wait()
    loads[1].wait()
    for side, own in ((0, k_ref), (1, v_ref)):
        kept = ((level1, 0), (near_rows, 0), (near_rows, 64), (near_rows, 96))
        for c in range(3):
            lanes = slice(c * 128, c * 128 + 128)
            steps, upper = steps_ref.at[3 * side + c], upper_ref.at[3 * side + c]
            steps[...] = own[:, lanes].astype(F32)
            count = 256
            for level in range(8):
                count //= 2
                rows = (steps[pl.ds(0, count, stride=2), :] + steps[pl.ds(1, count, stride=2), :]) * 0.5
                low = rows.astype(BF)
                rows = low.astype(F32)
                if level < 4:
                    ref, start = kept[level]
                    ref[side, start:start + count, lanes] = low
                else:
                    at = (0, 8, 12, 14)[level - 4]
                    upper[at:at + count, :] = rows
                if level < 7:
                    steps[0:count, :] = rows
            upper[15:16, :] = jnp.zeros((1, 128), F32)
            near_rows[side, 112:128, lanes] = upper[...].astype(BF)
    ug[lo] = near_rows[core, 112:128, :]

    pl.semaphore_wait(barrier, NEAR - 1 + FAR - 1 + 1)

    for b in reversed(range(NEAR_BITS)):
        each(1 << b, lo, lambda j, b=b: send(
            near_rows.at[near_peer(b, j) % 2, pl.ds(112, 16)], ug.at[lo], f1_s.at[0], f1_r.at[0],
            near_id(near_peer(b, j))))
    each(2, lo, lambda j: send(
        near_rows.at[j, pl.ds(64, 32)],
        far.at[j, pl.ds(pl.multiple_of(64 + core * 32, 16), 32)], f1_s.at[1], f1_r.at[1], near_id(near_peer(1, j))))
    each(4, lo, lambda j: send(
        near_rows.at[j % 2, pl.ds(96, 16)],
        far.at[j % 2, pl.ds(pl.multiple_of(128 + lo % 4 * 16, 16), 16)], f1_s.at[1], f1_r.at[1],
        near_id(near_peer(2, j))))
    partner = near_id(sibling(lo))
    send(near_rows.at[:, pl.ds(0, 64)], far.at[:, pl.ds(0, 64)], pair_s.at[0], pair_r.at[0], partner)


    lane_low = iota((128, 128), 1) < HEAD
    masks = (where_one(lane_low, 1.0), where_one(jnp.logical_not(lane_low), 1.0))

    def local_rows(own, i, p, side):
        lanes = slice(i * 128, i * 128 + 128)
        return jnp.concatenate(
            [own[p * 128:p * 128 + 128, lanes], level1[side, 64 * (1 - p):64 * (1 - p) + 64, lanes]], axis=0)

    loads[3].wait()
    loads[4].wait()
    for i in range(3):
        for p in range(2):
            part = q_ref[p * 128:p * 128 + 128, i * 128:i * 128 + 128]
            for h in range(2):
                at = p * 256 + h * 128
                bdq[i, at:at + 128, :] = part * masks[h]
        for p in range(2):
            probs[i, KEYS:KEYS + 192, p * 256:p * 256 + 256] = mm_nt(
                local_rows(k_ref, i, p, 0), bdq[i, p * 256:p * 256 + 256, :])

    landed_in(ug.at[pl.ds(0, NEAR - 1)], f1_r.at[0])
    gathered = ug[...].reshape(NEAR * 16, 384)
    a = iota((128, 128), 0)
    source = jnp.where(
        a < 64, a // 8 * 16 + a % 8,
        jnp.where(a < 96, (a - 64) // 4 * 16 + 8 + a % 4,
                  jnp.where(a < 112, (a - 96) // 2 * 16 + 12 + a % 2, (a - 112) * 16 + 14)))
    levels = mm(where_one(iota((128, 128), 1) == source, 1.0), gathered)
    up[...] = levels[0:112].astype(BF)
    up_f32[...] = levels[112:120]

    each(8, hi, lambda j: send(
        up_f32, far_f32.at[pl.ds(pl.multiple_of(hi % 8 * 8, 8), 8)], f2_s.at[1], f2_r.at[1], far_id(far_peer(3, j))))
    for b in reversed(range(3)):
        r = BLOCK >> b
        each(1 << b, hi, lambda j, b=b, r=r: send(
            up.at[pl.ds((0, 64, 96)[b], r)],
            far.at[core, pl.ds(pl.multiple_of((3 + b) * BLOCK + hi % (1 << b) * r, 16), r)],
            f2_s.at[0], f2_r.at[0], far_id(far_peer(b, j))))

    loads[2].wait()
    to_mp = pltpu.make_async_remote_copy(
        src_ref=go_ref, dst_ref=fg.at[mp], send_sem=mp_s.at[0], recv_sem=mp_r.at[0],
        device_id=mp_id, device_id_type=MESH)
    to_mp.start()
    fg[mp] = go_ref[...]

    for i in range(3):
        for p in range(2):
            k_loc_t[i, p] = local_rows(k_ref, i, p, 0).T
            v_loc_t[i, p] = local_rows(v_ref, i, p, 1).T

    at_row, at_col = iota((64, 256), 0), iota((64, 256), 1)
    spread = jnp.zeros((64, 256), F32)
    for b in range(FAR_BITS):
        hit = (at_col // 64 == b) & (at_row // (1 << b) == at_col % (64 >> b))
        spread = jnp.where(hit, 0.5 ** b, spread)
    to_group[...] = spread.astype(BF)
    at_row, at_col = iota((192, 64), 0), iota((192, 64), 1)
    spread = jnp.zeros((192, 64), F32)
    for b in range(NEAR_BITS):
        base = sibling(lo // (1 << b)) * (1 << b)
        hit = (at_row // 64 == b) & (at_col == 8 * base + at_row % 64 // (8 >> b))
        spread = jnp.where(hit, 0.5 ** (3 - b), spread)
    to_near[...] = spread.astype(BF)
    at_row, at_col = iota((256, 320), 0), iota((256, 320), 1)
    hits = (
        (at_col < 64) & (at_row // 4 == at_col),
        (at_col >= 64) & (at_col < 96) & (at_row // 8 == at_col - 64),
        (at_col >= 96) & (at_col < 128) & (at_row // 16 == at_col % 16),
        (at_col >= 128) & (at_col < 192) & (8 * lo + at_row // 32 == at_col - 128),
        (at_col >= 192) & (at_row // 2 == at_col - 192),
    )
    spread = jnp.zeros((256, 320), F32)
    for hit, weight in zip(hits, (0.25, 0.125, 0.0625, 0.03125, 0.5)):
        spread = jnp.where(hit, weight, spread)
    to_rows[...] = spread.astype(BF)

    landed_in(far_f32, f2_r.at[1])
    far[core, 384:448, :] = far_f32[...].astype(BF)
    landed_in(far.at[core, pl.ds(192, 192)], f2_r.at[0])
    send(far.at[core, pl.ds(192, 256)], far.at[core, pl.ds(192, 256)], pair_s.at[2], pair_r.at[2], partner)
    landed_in(far.at[core, pl.ds(64, 128)], f1_r.at[1])
    send(far.at[core, pl.ds(64, 128)], far.at[core, pl.ds(64, 128)], pair_s.at[1], pair_r.at[1], partner)
    landed_in(far.at[:, pl.ds(0, 64)], pair_r.at[0])
    landed_in(far.at[1 - core, pl.ds(64, 128)], pair_r.at[1])
    for i in range(3):
        probs[i, 0:192, :] = mm_nt(far[0, 0:192, i * 128:i * 128 + 128], bdq[i])

    landed_in(far.at[1 - core, pl.ds(192, 256)], pair_r.at[2])

    unit = HEAD ** -0.5 * 1.4426950408889634
    for i in range(3):
        probs[i, 192:KEYS, :] = mm_nt(far[0, 192:KEYS, i * 128:i * 128 + 128], bdq[i])
        v_far_t = far[1, :, i * 128:i * 128 + 128].T
        for p in range(2):
            for h in range(2):
                lanes = slice(p * 256 + h * 128, p * 256 + h * 128 + 128)
                scores = probs[i, :, lanes] * unit
                largest = jnp.max(scores, axis=0, keepdims=True)
                weights = jnp.exp2(scores - largest)
                weights = weights * (1.0 / jnp.sum(weights, axis=0, keepdims=True))
                probs[i, :, lanes] = weights
                low = weights.astype(BF)
                part = mm(v_far_t[h * 64:h * 64 + 64], low[:KEYS]) + mm(v_loc_t[i, p, h * 64:h * 64 + 64], low[KEYS:])
                attn_t[i * 128 + h * 64:i * 128 + h * 64 + 64, p * 128:p * 128 + 128] = part.astype(BF)

    attn = attn_t[...].T
    lo_send[...] = mm(attn, w_ref[:, pl.ds(pl.multiple_of((1 - mp) * 384, 128), 384)]).astype(BF)
    to_lo = pltpu.make_async_remote_copy(
        src_ref=lo_send, dst_ref=lo_land, send_sem=mp_s.at[1], recv_sem=mp_r.at[1],
        device_id=mp_id, device_id_type=MESH)
    to_lo.start()

    def chunk_of(terms, f):
        pieces = [terms[CHUNK * f:CHUNK * f + CHUNK, c * 128:c * 128 + 128] for c in range(3)]
        return jnp.concatenate(pieces + [jnp.zeros((8, 128), F32)], axis=0)

    landed_in(fg.at[1 - mp], mp_r.at[0])
    terms = mm(attn_t[...], fg[1 - core])
    for f in range(FAR):
        gw_x[f] = chunk_of(terms, f).astype(BF)
    send(gw_x, gw_pl, pair_s.at[3], pair_r.at[3], partner)

    terms = mm(attn_t[...], fg[core])
    for f in range(FAR):
        gw_own[f] = chunk_of(terms, f)
    landed_in(gw_pl, pair_r.at[3])
    gw_send[...] = (gw_own[...] + gw_pl[...].astype(F32)).astype(BF)
    gw_land[hi] = gw_send[hi]
    for b in reversed(range(FAR_BITS)):
        each(1 << b, hi, lambda j, b=b: send(
            gw_send.at[far_peer(b, j)], gw_land.at[hi], gw_s.at[0], gw_r.at[0], far_id(far_peer(b, j))))

    grad_attn = (mm_nt(fg[0], w_ref[:, 0:384]) + mm_nt(fg[1], w_ref[:, 384:768])).astype(BF)
    for i in range(3):
        lanes_i = slice(i * 128, i * 128 + 128)
        for p in range(2):
            part = grad_attn[p * 128:p * 128 + 128, lanes_i]
            for h in range(2):
                at = p * 256 + h * 128
                bdo[i, at:at + 128, :] = part * masks[h]
    for i in range(3):
        lanes_i = slice(i * 128, i * 128 + 128)
        gp_far = mm_nt(far[1, :, lanes_i], bdo[i])
        k_far_t = far[0, :, lanes_i].T
        d_scores, p_low = [], []
        for p in range(2):
            gp_loc = mm_nt(local_rows(v_ref, i, p, 1), bdo[i, p * 256:p * 256 + 256, :])
            ds_half, pl_half = [], []
            for h in range(2):
                lanes = slice(p * 256 + h * 128, p * 256 + h * 128 + 128)
                weights = probs[i, :, lanes]
                grads = jnp.concatenate([gp_far[:, lanes], gp_loc[:, h * 128:h * 128 + 128]], axis=0)
                centre = jnp.sum(weights * grads, axis=0, keepdims=True)
                ds = (weights * (grads - centre) * HEAD ** -0.5).astype(BF)
                part = mm(k_far_t[h * 64:h * 64 + 64], ds[:KEYS]) + mm(k_loc_t[i, p, h * 64:h * 64 + 64], ds[KEYS:])
                dq_t[i * 128 + h * 64:i * 128 + h * 64 + 64, p * 128:p * 128 + 128] = part
                ds_half.append(ds)
                pl_half.append(weights.astype(BF))
            ds_p = jnp.concatenate(ds_half, axis=1)
            pl_p = jnp.concatenate(pl_half, axis=1)
            d_scores.append(ds_p)
            p_low.append(pl_p)
        for side, left, right in ((0, d_scores, bdq), (1, p_low, bdo)):
            grads = mm(jnp.concatenate([part[:KEYS] for part in left], axis=1), right[i])
            d_far[side, :, lanes_i] = grads
            d_x[side, :, lanes_i] = grads[64:KEYS].astype(BF)
            for p in range(2):
                grads = mm(left[p][KEYS:], right[i, p * 256:p * 256 + 256, :])
                d_loc[side, p * 128:p * 128 + 128, lanes_i] = grads[0:128]
                d_l1[side, 64 * (1 - p):64 * (1 - p) + 64, lanes_i] = grads[128:192].astype(BF)

    send(d_x.at[1 - core], d_land, pair_s.at[4], pair_r.at[4], partner)

    landed_in(gw_land.at[pl.ds(0, FAR - 1)], gw_r.at[0])
    total = gw_land[0].astype(F32)
    for f in range(1, FAR):
        total = total + gw_land[f].astype(F32)
    gw_part[...] = total.astype(BF)
    gw_ar[depth] = gw_part[...]
    for t in range(1, 4):
        other = (depth + t) % 4
        send(gw_part, gw_ar.at[depth], gw_s.at[1], gw_r.at[1], near_id(other * 2 + core))

    landed_in(d_land, pair_r.at[4])
    total = d_far[core, 64:KEYS, :] + d_land[...].astype(F32)
    d_send[...] = total[128:320].astype(BF)
    d_f32[...] = total[320:384]
    d_near[...] = total[0:128]
    each(8, hi, lambda j: send(
        d_f32.at[pl.ds(pl.multiple_of(j * 8, 8), 8)], r1_f32.at[pl.ds(pl.multiple_of(hi % 8 * 8, 8), 8)],
        r1_s.at[1], r1_r.at[1], far_id(far_peer(3, j))))
    for b in reversed(range(3)):
        r = BLOCK >> b
        each(1 << b, hi, lambda j, b=b, r=r: send(
            d_send.at[pl.ds(pl.multiple_of(b * BLOCK + j * r, 16), r)],
            r1_land.at[pl.ds(pl.multiple_of(b * BLOCK + hi % (1 << b) * r, 16), r)],
            r1_s.at[0], r1_r.at[0], far_id(far_peer(b, j))))

    landed_in(gw_ar.at[pl.ds(0, 3)], gw_r.at[1])
    total = gw_ar[0].astype(F32)
    for e in range(1, 4):
        total = total + gw_ar[e].astype(F32)
    gw_all[core, hi] = total.astype(BF)
    for b in range(FAR_BITS):
        each(1 << b, hi, lambda j, b=b: send(
            gw_all.at[core, hi], gw_all.at[core, hi], gw_s.at[2], gw_r.at[2 + b // 3], far_id(far_peer(b, j))))

    dq_out[...] = dq_t[...].T.astype(BF)
    stores[1].start()
    mine = mm(attn, w_ref[:, pl.ds(pl.multiple_of(mp * 384, 128), 384)])

    landed_in(r1_land, r1_r.at[0])
    landed_in(r1_f32, r1_r.at[1])
    landed = jnp.concatenate([r1_land[...], r1_f32[...].astype(BF)], axis=0)
    group_grad = mm(to_group[...], landed).astype(BF)
    gg[core] = group_grad
    gg[1 - core] = jnp.zeros((64, 384), BF)
    spread = mm(to_near[...], group_grad)
    msg[...] = (d_near[...] + spread[64:192]).astype(BF)
    msg0[core] = (d_far[core, 0:64, :] + spread[0:64]).astype(BF)
    msg0[1 - core] = d_far[1 - core, 0:64, :].astype(BF)

    each(2, lo, lambda j: send(
        msg.at[pl.ds(pl.multiple_of(j * 32, 16), 32)], r2_land.at[core, pl.ds(64, 32)],
        r2_s.at[0], r2_r.at[0], near_id(near_peer(1, j))))
    each(4, lo, lambda j: send(
        msg.at[pl.ds(pl.multiple_of(64 + j * 16, 16), 16)],
        r2_land.at[core, pl.ds(pl.multiple_of(96 + depth % 2 * 16, 16), 16)],
        r2_s.at[0], r2_r.at[0], near_id(near_peer(2, j))))
    send(msg0, r2_land.at[:, pl.ds(0, 64)], pair_s.at[5], pair_r.at[5], partner)

    landed_in(gw_all.at[core, pl.ds(0, 7)], gw_r.at[2])
    eight = pl.multiple_of(hi // 8 * 8, 8)
    send(gw_all.at[core, pl.ds(eight, 8)], gw_all.at[core, pl.ds(eight, 8)], pair_s.at[6], pair_r.at[6], partner)
    landed_in(gw_all.at[core, pl.ds(0, 8)], gw_r.at[3])
    eight = pl.multiple_of(sibling(hi // 8) * 8, 8)
    send(gw_all.at[core, pl.ds(eight, 8)], gw_all.at[core, pl.ds(eight, 8)], pair_s.at[7], pair_r.at[7], partner)

    landed_in(r2_land.at[:, pl.ds(64, 64)], r2_r.at[0])
    landed_in(r2_land.at[:, pl.ds(0, 64)], pair_r.at[5])
    for side, out in ((0, dk_out), (1, dv_out)):
        terms = jnp.concatenate([r2_land[side], gg[side], d_l1[side]], axis=0)
        out[...] = (d_loc[side] + mm(to_rows[...], terms)).astype(BF)
        stores[2 + side].start()

    landed_in(lo_land, mp_r.at[1])
    lo_out[...] = (mine + lo_land[...].astype(F32)).astype(BF)
    stores[0].start()

    landed_in(gw_all.at[1 - core, pl.ds(0, 8)], pair_r.at[6])
    landed_in(gw_all.at[1 - core, pl.ds(0, 8)], pair_r.at[7])
    stores[4].start()

    landed_in(ug.at[pl.ds(0, NEAR - 1)], f1_s.at[0])
    landed_in(far.at[core, pl.ds(64, 128)], f1_s.at[1])
    landed_in(far.at[core, pl.ds(192, 192)], f2_s.at[0])
    landed_in(far_f32, f2_s.at[1])
    landed_in(r1_land, r1_s.at[0])
    landed_in(r1_f32, r1_s.at[1])
    landed_in(msg, r2_s.at[0])
    landed_in(gw_land.at[pl.ds(0, FAR - 1)], gw_s.at[0])
    landed_in(gw_ar.at[pl.ds(0, 3)], gw_s.at[1])
    landed_in(gw_land.at[pl.ds(0, FAR - 1)], gw_s.at[2])
    landed_in(msg0, pair_s.at[0])
    landed_in(msg, pair_s.at[1])
    landed_in(far.at[core, pl.ds(192, 256)], pair_s.at[2])
    landed_in(gw_x, pair_s.at[3])
    landed_in(d_land, pair_s.at[4])
    landed_in(msg0, pair_s.at[5])
    landed_in(gw_all.at[core, pl.ds(0, 8)], pair_s.at[6])
    landed_in(gw_all.at[core, pl.ds(0, 8)], pair_s.at[7])
    to_mp.wait_send()
    to_lo.wait_send()
    for store in stores:
        store.wait()


def hand_over(*refs):
    given, out, held, whole, sem = refs[0:5], refs[5:10], refs[10:15], refs[15], refs[16]
    first = [pltpu.make_async_copy(given[n], held[n], sem.at[n]) for n in range(4)]
    halves = [pltpu.make_async_copy(given[4].at[n], held[4].at[n], sem.at[8 + n]) for n in range(2)]
    second = [pltpu.make_async_copy(held[n], out[n], sem.at[4 + n]) for n in range(4)]
    for copy in halves + first:
        copy.start()
    for side in range(2):
        halves[side].wait()
        for f in range(FAR):
            part = held[4][side, f].astype(F32)
            for c in range(3):
                at = side * 384 + c * 128
                whole[CHUNK * f:CHUNK * f + CHUNK, at:at + 128] = part[c * CHUNK:c * CHUNK + CHUNK]
        columns = pl.ds(side * 384, 384)
        second.append(pltpu.make_async_copy(whole.at[:, columns], out[4].at[:, columns], sem.at[10 + side]))
        second[-1].start()
    for n in range(4):
        first[n].wait()
        second[n].start()
    for copy in second:
        copy.wait()


def on_device(query_rows, key_rows, value_rows, w_output, grad_output):
    vm = pltpu.VMEM
    dma = pltpu.SemaphoreType.DMA
    piece = (80, 128)
    scratch = [
        vm((256, 384), BF), vm((256, 384), BF), vm((256, 384), BF), vm((256, 384), BF),
        vm((256, 384), BF), vm((256, 384), BF), vm((256, 384), BF), vm((384, 768), BF), vm((256, 384), BF),
        vm((6, 256, 128), F32),
        vm((6, 16, 128), F32),
        vm((64, 256), BF),
        vm((192, 64), BF),
        vm((256, 320), BF),
        vm((3, 2, 128, 192), BF),
        vm((3, 2, 128, 192), BF),
        vm((2, 128, 384), BF),
        vm((2, 128, 384), BF),
        vm((2, KEYS, 384), BF),
        vm((64, 384), F32),
        vm((NEAR, 16, 384), BF),
        vm((112, 384), BF),
        vm((8, 384), F32),
        vm((2, 256, 384), BF),
        vm((3, 512, 128), BF),
        vm((3, 512, 128), BF),
        vm((3, KEYS + 192, 512), F32),
        vm((384, 256), BF),
        vm((384, 256), F32),
        vm((2, KEYS, 384), F32),
        vm((2, 384, 384), BF),
        vm((384, 384), BF),
        vm((128, 384), F32),
        vm((192, 384), BF),
        vm((64, 384), F32),
        vm((192, 384), BF),
        vm((64, 384), F32),
        vm((2, 64, 384), BF),
        vm((2, 64, 384), BF),
        vm((128, 384), BF),
        vm((2, 128, 384), BF),
        vm((2, 256, 384), F32),
        vm((2, 128, 384), BF),
        vm((FAR,) + piece, BF),
        vm((FAR,) + piece, BF),
        vm((FAR,) + piece, F32),
        vm((FAR,) + piece, BF),
        vm((FAR,) + piece, BF),
        vm(piece, BF),
        vm((4,) + piece, BF),
        vm((2, FAR) + piece, BF),
        vm((256, 384), BF),
        vm((256, 384), BF),
        dma((5,)),
        dma((5,)),
        dma((2,)), dma((2,)),
        dma((2,)), dma((2,)),
        dma((2,)), dma((2,)),
        dma((1,)), dma((1,)),
        dma((3,)), dma((4,)),
        dma((8,)), dma((8,)),
        dma((2,)), dma((2,)),
    ]
    rows = jax.ShapeDtypeStruct((256, 384), BF)
    chunks = jax.ShapeDtypeStruct((2, FAR) + piece, BF)
    in_hbm = pl.BlockSpec(memory_space=pltpu.HBM)
    results = pl.pallas_call(
        kernel,
        out_shape=(rows, rows, rows, rows, chunks),
        in_specs=[in_hbm] * 5,
        out_specs=(in_hbm,) * 5,
        scratch_shapes=scratch,
        compiler_params=pltpu.CompilerParams(
            collective_id=0, has_side_effects=True, vmem_limit_bytes=58 * 1024 * 1024),
        cost_estimate=pl.CostEstimate(flops=1_200_000_000, bytes_accessed=4_000_000, transcendentals=1_000_000),
    )(query_rows, key_rows, value_rows, w_output, grad_output)
    held = [vm((256, 384), BF)] * 4 + [vm((2, FAR) + piece, BF), vm((384, 768), F32)]
    return pl.pallas_call(
        hand_over,
        out_shape=(rows, rows, rows, rows, jax.ShapeDtypeStruct((384, 768), F32)),
        in_specs=[in_hbm] * 5,
        out_specs=(in_hbm,) * 5,
        scratch_shapes=held + [dma((12,))],
        compiler_params=pltpu.CompilerParams(vmem_limit_bytes=58 * 1024 * 1024),
    )(*results)


def solution(mesh):
    placed = (P("ctx", "mp"), P("ctx", "mp"), P("ctx", "mp"), P("mp", None), P("ctx", "mp"))
    return jax.shard_map(
        on_device,
        mesh=mesh,
        in_specs=placed,
        out_specs=(P("ctx", "mp"), P("ctx", "mp"), P("ctx", "mp"), P("ctx", "mp"), P("mp", None)),
        check_vma=False,
    )
```

```python
import jax
import jax.numpy as jnp
from jax import lax
from jax.experimental import pallas as pl
from jax.experimental.pallas import tpu as pltpu
from jax.sharding import PartitionSpec as P

HEAD = 64
BLOCK = 64
NEAR = 8
NEAR_BITS = 3
FAR = 16
FAR_BITS = 4
KEYS = (NEAR_BITS + FAR_BITS) * BLOCK
CHUNK = 24
MESH = pl.DeviceIdType.MESH
BF = jnp.bfloat16
F32 = jnp.float32


def iota(shape, axis):
    return lax.broadcasted_iota(jnp.int32, shape, axis)


def where_one(condition, weight):
    return jnp.where(condition, weight, 0.0).astype(BF)


def mm(a, b):
    return jnp.dot(a, b, preferred_element_type=F32)


def mm_nt(a, b):
    return lax.dot_general(a, b, (((1,), (1,)), ((), ())), preferred_element_type=F32)


def sibling(index):
    return index + 1 - 2 * (index % 2)


def kernel(
    q_hbm, k_hbm, v_hbm, w_hbm, go_hbm,
    lo_hbm, dq_hbm, dk_hbm, dv_hbm, gw_hbm,
    lo_out, dq_out, dk_out, dv_out,
    q_ref, k_ref, v_ref, w_ref, go_ref,
    steps_ref, upper_ref, k_far_t, to_group, to_near, to_rows, k_loc_t, v_loc_t, near_rows, level1, far, far_f32, ug, up, up_f32, fg, bdq, bdo, probs, attn_t, dq_t,
    d_far, d_x, d_land, d_near, d_send, d_f32, r1_land, r1_f32, gg, msg0, msg, r2_land, d_loc, d_l1,
    gw_x, gw_pl, gw_own, gw_send, gw_land, gw_part, gw_ar, gw_all, lo_send, lo_land,
    ld, st, f1_s, f1_r, f2_s, f2_r, r1_s, r1_r, r2_s, r2_r, gw_s, gw_r, pair_s, pair_r, mp_s, mp_r,
):
    place = lax.axis_index("ctx")
    mp = lax.axis_index("mp")
    hi = place // NEAR
    lo = place % NEAR
    core = lo % 2
    depth = lo // 2

    def near_id(e):
        return (hi * NEAR + e, mp)

    def far_id(f):
        return (f * NEAR + lo, mp)

    mp_id = (place, 1 - mp)

    def send(src, dst, s, r, to):
        pltpu.make_async_remote_copy(
            src_ref=src, dst_ref=dst, send_sem=s, recv_sem=r, device_id=to, device_id_type=MESH).start()

    def near_peer(b, j):
        return sibling(lo // (1 << b)) * (1 << b) + j

    def far_peer(b, j):
        return sibling(hi // (1 << b)) * (1 << b) + j

    def each(n, mine, body):
        if n <= 8:
            for j in range(n):
                body((j + mine) % n)
        else:
            def step(t, c):
                body((t + mine) % n)
                return c
            lax.fori_loop(0, n, step, 0)

    def landed_in(ref, sem):
        pltpu.make_async_copy(ref, ref, sem).wait()

    loads = [pltpu.make_async_copy(src, dst, ld.at[n]) for n, (src, dst) in enumerate(
        ((k_hbm, k_ref), (v_hbm, v_ref), (go_hbm, go_ref), (q_hbm, q_ref), (w_hbm, w_ref)))]
    for load in loads:
        load.start()
    stores = [pltpu.make_async_copy(src, dst, st.at[n]) for n, (src, dst) in enumerate(
        ((lo_out, lo_hbm), (dq_out, dq_hbm), (dk_out, dk_hbm), (dv_out, dv_hbm), (gw_all, gw_hbm)))]
    barrier = pltpu.get_barrier_semaphore()
    for b in range(NEAR_BITS):
        each(1 << b, lo, lambda j, b=b: pl.semaphore_signal(
            barrier, inc=1, device_id=near_id(near_peer(b, j)), device_id_type=MESH))
    for b in range(FAR_BITS):
        each(1 << b, hi, lambda j, b=b: pl.semaphore_signal(
            barrier, inc=1, device_id=far_id(far_peer(b, j)), device_id_type=MESH))
    pl.semaphore_signal(barrier, inc=1, device_id=mp_id, device_id_type=MESH)

    loads[0].wait()
    loads[1].wait()
    for side, own in ((0, k_ref), (1, v_ref)):
        kept = ((level1, 0), (near_rows, 0), (near_rows, 64), (near_rows, 96))
        for c in range(3):
            lanes = slice(c * 128, c * 128 + 128)
            steps, upper = steps_ref.at[3 * side + c], upper_ref.at[3 * side + c]
            steps[...] = own[:, lanes].astype(F32)
            count = 256
            for level in range(8):
                count //= 2
                rows = (steps[pl.ds(0, count, stride=2), :] + steps[pl.ds(1, count, stride=2), :]) * 0.5
                low = rows.astype(BF)
                rows = low.astype(F32)
                if level < 4:
                    ref, start = kept[level]
                    ref[side, start:start + count, lanes] = low
                else:
                    at = (0, 8, 12, 14)[level - 4]
                    upper[at:at + count, :] = rows
                if level < 7:
                    steps[0:count, :] = rows
            upper[15:16, :] = jnp.zeros((1, 128), F32)
            near_rows[side, 112:128, lanes] = upper[...].astype(BF)
    ug[lo] = near_rows[core, 112:128, :]

    pl.semaphore_wait(barrier, NEAR - 1 + FAR - 1 + 1)

    for b in reversed(range(NEAR_BITS)):
        each(1 << b, lo, lambda j, b=b: send(
            near_rows.at[near_peer(b, j) % 2, pl.ds(112, 16)], ug.at[lo], f1_s.at[0], f1_r.at[0],
            near_id(near_peer(b, j))))
    each(2, lo, lambda j: send(
        near_rows.at[j, pl.ds(64, 32)],
        far.at[j, pl.ds(pl.multiple_of(64 + core * 32, 16), 32)], f1_s.at[1], f1_r.at[1], near_id(near_peer(1, j))))
    each(4, lo, lambda j: send(
        near_rows.at[j % 2, pl.ds(96, 16)],
        far.at[j % 2, pl.ds(pl.multiple_of(128 + lo % 4 * 16, 16), 16)], f1_s.at[1], f1_r.at[1],
        near_id(near_peer(2, j))))
    partner = near_id(sibling(lo))
    send(near_rows.at[:, pl.ds(0, 64)], far.at[:, pl.ds(0, 64)], pair_s.at[0], pair_r.at[0], partner)


    lane_low = iota((128, 128), 1) < HEAD
    masks = (where_one(lane_low, 1.0), where_one(jnp.logical_not(lane_low), 1.0))

    def local_rows(own, i, p, side):
        lanes = slice(i * 128, i * 128 + 128)
        return jnp.concatenate(
            [own[p * 128:p * 128 + 128, lanes], level1[side, 64 * (1 - p):64 * (1 - p) + 64, lanes]], axis=0)

    loads[3].wait()
    loads[4].wait()
    for i in range(3):
        for p in range(2):
            part = q_ref[p * 128:p * 128 + 128, i * 128:i * 128 + 128]
            for h in range(2):
                at = p * 256 + h * 128
                bdq[i, at:at + 128, :] = part * masks[h]
        for p in range(2):
            probs[i, KEYS:KEYS + 192, p * 256:p * 256 + 256] = mm_nt(
                local_rows(k_ref, i, p, 0), bdq[i, p * 256:p * 256 + 256, :])

    landed_in(ug.at[pl.ds(0, NEAR - 1)], f1_r.at[0])
    gathered = ug[...].reshape(NEAR * 16, 384)
    a = iota((128, 128), 0)
    source = jnp.where(
        a < 64, a // 8 * 16 + a % 8,
        jnp.where(a < 96, (a - 64) // 4 * 16 + 8 + a % 4,
                  jnp.where(a < 112, (a - 96) // 2 * 16 + 12 + a % 2, (a - 112) * 16 + 14)))
    levels = mm(where_one(iota((128, 128), 1) == source, 1.0), gathered)
    up[...] = levels[0:112].astype(BF)
    up_f32[...] = levels[112:120]

    each(8, hi, lambda j: send(
        up_f32, far_f32.at[pl.ds(pl.multiple_of(hi % 8 * 8, 8), 8)], f2_s.at[1], f2_r.at[1], far_id(far_peer(3, j))))
    for b in reversed(range(3)):
        r = BLOCK >> b
        each(1 << b, hi, lambda j, b=b, r=r: send(
            up.at[pl.ds((0, 64, 96)[b], r)],
            far.at[core, pl.ds(pl.multiple_of((3 + b) * BLOCK + hi % (1 << b) * r, 16), r)],
            f2_s.at[0], f2_r.at[0], far_id(far_peer(b, j))))

    loads[2].wait()
    to_mp = pltpu.make_async_remote_copy(
        src_ref=go_ref, dst_ref=fg.at[mp], send_sem=mp_s.at[0], recv_sem=mp_r.at[0],
        device_id=mp_id, device_id_type=MESH)
    to_mp.start()
    fg[mp] = go_ref[...]

    for i in range(3):
        for p in range(2):
            k_loc_t[i, p] = local_rows(k_ref, i, p, 0).T
            v_loc_t[i, p] = local_rows(v_ref, i, p, 1).T

    at_row, at_col = iota((64, 256), 0), iota((64, 256), 1)
    spread = jnp.zeros((64, 256), F32)
    for b in range(FAR_BITS):
        hit = (at_col // 64 == b) & (at_row // (1 << b) == at_col % (64 >> b))
        spread = jnp.where(hit, 0.5 ** b, spread)
    to_group[...] = spread.astype(BF)
    at_row, at_col = iota((192, 64), 0), iota((192, 64), 1)
    spread = jnp.zeros((192, 64), F32)
    for b in range(NEAR_BITS):
        base = sibling(lo // (1 << b)) * (1 << b)
        hit = (at_row // 64 == b) & (at_col == 8 * base + at_row % 64 // (8 >> b))
        spread = jnp.where(hit, 0.5 ** (3 - b), spread)
    to_near[...] = spread.astype(BF)
    at_row, at_col = iota((256, 320), 0), iota((256, 320), 1)
    hits = (
        (at_col < 64) & (at_row // 4 == at_col),
        (at_col >= 64) & (at_col < 96) & (at_row // 8 == at_col - 64),
        (at_col >= 96) & (at_col < 128) & (at_row // 16 == at_col % 16),
        (at_col >= 128) & (at_col < 192) & (8 * lo + at_row // 32 == at_col - 128),
        (at_col >= 192) & (at_row // 2 == at_col - 192),
    )
    spread = jnp.zeros((256, 320), F32)
    for hit, weight in zip(hits, (0.25, 0.125, 0.0625, 0.03125, 0.5)):
        spread = jnp.where(hit, weight, spread)
    to_rows[...] = spread.astype(BF)

    landed_in(far_f32, f2_r.at[1])
    far[core, 384:448, :] = far_f32[...].astype(BF)
    landed_in(far.at[core, pl.ds(192, 192)], f2_r.at[0])
    send(far.at[core, pl.ds(192, 256)], far.at[core, pl.ds(192, 256)], pair_s.at[2], pair_r.at[2], partner)
    landed_in(far.at[core, pl.ds(64, 128)], f1_r.at[1])
    send(far.at[core, pl.ds(64, 128)], far.at[core, pl.ds(64, 128)], pair_s.at[1], pair_r.at[1], partner)
    landed_in(far.at[:, pl.ds(0, 64)], pair_r.at[0])
    landed_in(far.at[1 - core, pl.ds(64, 128)], pair_r.at[1])
    for i in range(3):
        probs[i, 0:192, :] = mm_nt(far[0, 0:192, i * 128:i * 128 + 128], bdq[i])

    landed_in(far.at[1 - core, pl.ds(192, 256)], pair_r.at[2])

    unit = HEAD ** -0.5 * 1.4426950408889634
    for i in range(3):
        probs[i, 192:KEYS, :] = mm_nt(far[0, 192:KEYS, i * 128:i * 128 + 128], bdq[i])
        v_far_t = far[1, :, i * 128:i * 128 + 128].T
        for p in range(2):
            for h in range(2):
                lanes = slice(p * 256 + h * 128, p * 256 + h * 128 + 128)
                scores = probs[i, :, lanes] * unit
                largest = jnp.max(scores, axis=0, keepdims=True)
                weights = jnp.exp2(scores - largest)
                weights = weights * (1.0 / jnp.sum(weights, axis=0, keepdims=True))
                probs[i, :, lanes] = weights
                low = weights.astype(BF)
                part = mm(v_far_t[h * 64:h * 64 + 64], low[:KEYS]) + mm(v_loc_t[i, p, h * 64:h * 64 + 64], low[KEYS:])
                attn_t[i * 128 + h * 64:i * 128 + h * 64 + 64, p * 128:p * 128 + 128] = part.astype(BF)

    attn = attn_t[...].T
    lo_send[...] = mm(attn, w_ref[:, pl.ds(pl.multiple_of((1 - mp) * 384, 128), 384)]).astype(BF)
    to_lo = pltpu.make_async_remote_copy(
        src_ref=lo_send, dst_ref=lo_land, send_sem=mp_s.at[1], recv_sem=mp_r.at[1],
        device_id=mp_id, device_id_type=MESH)
    to_lo.start()

    def chunk_of(terms, f):
        pieces = [terms[CHUNK * f:CHUNK * f + CHUNK, c * 128:c * 128 + 128] for c in range(3)]
        return jnp.concatenate(pieces + [jnp.zeros((8, 128), F32)], axis=0)

    for i in range(3):
        k_far_t[i] = far[0, :, i * 128:i * 128 + 128].T
    landed_in(fg.at[1 - mp], mp_r.at[0])
    terms = mm(attn_t[...], fg[1 - core])
    for f in range(FAR):
        gw_x[f] = chunk_of(terms, f).astype(BF)
    send(gw_x, gw_pl, pair_s.at[3], pair_r.at[3], partner)

    terms = mm(attn_t[...], fg[core])
    for f in range(FAR):
        gw_own[f] = chunk_of(terms, f)
    landed_in(gw_pl, pair_r.at[3])
    gw_send[...] = (gw_own[...] + gw_pl[...].astype(F32)).astype(BF)
    gw_land[hi] = gw_send[hi]
    for b in reversed(range(FAR_BITS)):
        each(1 << b, hi, lambda j, b=b: send(
            gw_send.at[far_peer(b, j)], gw_land.at[hi], gw_s.at[0], gw_r.at[0], far_id(far_peer(b, j))))

    grad_attn = (mm_nt(fg[0], w_ref[:, 0:384]) + mm_nt(fg[1], w_ref[:, 384:768])).astype(BF)
    for i in range(3):
        lanes_i = slice(i * 128, i * 128 + 128)
        for p in range(2):
            part = grad_attn[p * 128:p * 128 + 128, lanes_i]
            for h in range(2):
                at = p * 256 + h * 128
                bdo[i, at:at + 128, :] = part * masks[h]
    for i in range(3):
        lanes_i = slice(i * 128, i * 128 + 128)
        gp_far = mm_nt(far[1, :, lanes_i], bdo[i])
        d_scores, p_low = [], []
        for p in range(2):
            gp_loc = mm_nt(local_rows(v_ref, i, p, 1), bdo[i, p * 256:p * 256 + 256, :])
            ds_half, pl_half = [], []
            for h in range(2):
                lanes = slice(p * 256 + h * 128, p * 256 + h * 128 + 128)
                weights = probs[i, :, lanes]
                grads = jnp.concatenate([gp_far[:, lanes], gp_loc[:, h * 128:h * 128 + 128]], axis=0)
                centre = jnp.sum(weights * grads, axis=0, keepdims=True)
                ds = (weights * (grads - centre) * HEAD ** -0.5).astype(BF)
                part = mm(k_far_t[i, h * 64:h * 64 + 64], ds[:KEYS]) + mm(k_loc_t[i, p, h * 64:h * 64 + 64], ds[KEYS:])
                dq_t[i * 128 + h * 64:i * 128 + h * 64 + 64, p * 128:p * 128 + 128] = part
                ds_half.append(ds)
                pl_half.append(weights.astype(BF))
            ds_p = jnp.concatenate(ds_half, axis=1)
            pl_p = jnp.concatenate(pl_half, axis=1)
            d_scores.append(ds_p)
            p_low.append(pl_p)
        for side, left, right in ((0, d_scores, bdq), (1, p_low, bdo)):
            grads = mm(jnp.concatenate([part[:KEYS] for part in left], axis=1), right[i])
            d_far[side, :, lanes_i] = grads
            d_x[side, :, lanes_i] = grads[64:KEYS].astype(BF)
            for p in range(2):
                grads = mm(left[p][KEYS:], right[i, p * 256:p * 256 + 256, :])
                d_loc[side, p * 128:p * 128 + 128, lanes_i] = grads[0:128]
                d_l1[side, 64 * (1 - p):64 * (1 - p) + 64, lanes_i] = grads[128:192].astype(BF)

    send(d_x.at[1 - core], d_land, pair_s.at[4], pair_r.at[4], partner)

    landed_in(gw_land.at[pl.ds(0, FAR - 1)], gw_r.at[0])
    total = gw_land[0].astype(F32)
    for f in range(1, FAR):
        total = total + gw_land[f].astype(F32)
    gw_part[...] = total.astype(BF)
    gw_ar[depth] = gw_part[...]
    for t in range(1, 4):
        other = (depth + t) % 4
        send(gw_part, gw_ar.at[depth], gw_s.at[1], gw_r.at[1], near_id(other * 2 + core))

    landed_in(d_land, pair_r.at[4])
    total = d_far[core, 64:KEYS, :] + d_land[...].astype(F32)
    d_send[...] = total[128:320].astype(BF)
    d_f32[...] = total[320:384]
    d_near[...] = total[0:128]
    each(8, hi, lambda j: send(
        d_f32.at[pl.ds(pl.multiple_of(j * 8, 8), 8)], r1_f32.at[pl.ds(pl.multiple_of(hi % 8 * 8, 8), 8)],
        r1_s.at[1], r1_r.at[1], far_id(far_peer(3, j))))
    for b in reversed(range(3)):
        r = BLOCK >> b
        each(1 << b, hi, lambda j, b=b, r=r: send(
            d_send.at[pl.ds(pl.multiple_of(b * BLOCK + j * r, 16), r)],
            r1_land.at[pl.ds(pl.multiple_of(b * BLOCK + hi % (1 << b) * r, 16), r)],
            r1_s.at[0], r1_r.at[0], far_id(far_peer(b, j))))

    landed_in(gw_ar.at[pl.ds(0, 3)], gw_r.at[1])
    total = gw_ar[0].astype(F32)
    for e in range(1, 4):
        total = total + gw_ar[e].astype(F32)
    gw_all[core, hi] = total.astype(BF)
    for b in range(FAR_BITS):
        each(1 << b, hi, lambda j, b=b: send(
            gw_all.at[core, hi], gw_all.at[core, hi], gw_s.at[2], gw_r.at[2 + b // 3], far_id(far_peer(b, j))))

    dq_out[...] = dq_t[...].T.astype(BF)
    stores[1].start()
    mine = mm(attn, w_ref[:, pl.ds(pl.multiple_of(mp * 384, 128), 384)])

    landed_in(r1_land, r1_r.at[0])
    landed_in(r1_f32, r1_r.at[1])
    landed = jnp.concatenate([r1_land[...], r1_f32[...].astype(BF)], axis=0)
    group_grad = mm(to_group[...], landed).astype(BF)
    gg[core] = group_grad
    gg[1 - core] = jnp.zeros((64, 384), BF)
    spread = mm(to_near[...], group_grad)
    msg[...] = (d_near[...] + spread[64:192]).astype(BF)
    msg0[core] = (d_far[core, 0:64, :] + spread[0:64]).astype(BF)
    msg0[1 - core] = d_far[1 - core, 0:64, :].astype(BF)

    each(2, lo, lambda j: send(
        msg.at[pl.ds(pl.multiple_of(j * 32, 16), 32)], r2_land.at[core, pl.ds(64, 32)],
        r2_s.at[0], r2_r.at[0], near_id(near_peer(1, j))))
    each(4, lo, lambda j: send(
        msg.at[pl.ds(pl.multiple_of(64 + j * 16, 16), 16)],
        r2_land.at[core, pl.ds(pl.multiple_of(96 + depth % 2 * 16, 16), 16)],
        r2_s.at[0], r2_r.at[0], near_id(near_peer(2, j))))
    send(msg0, r2_land.at[:, pl.ds(0, 64)], pair_s.at[5], pair_r.at[5], partner)

    landed_in(gw_all.at[core, pl.ds(0, 7)], gw_r.at[2])
    eight = pl.multiple_of(hi // 8 * 8, 8)
    send(gw_all.at[core, pl.ds(eight, 8)], gw_all.at[core, pl.ds(eight, 8)], pair_s.at[6], pair_r.at[6], partner)
    landed_in(gw_all.at[core, pl.ds(0, 8)], gw_r.at[3])
    eight = pl.multiple_of(sibling(hi // 8) * 8, 8)
    send(gw_all.at[core, pl.ds(eight, 8)], gw_all.at[core, pl.ds(eight, 8)], pair_s.at[7], pair_r.at[7], partner)

    landed_in(r2_land.at[:, pl.ds(64, 64)], r2_r.at[0])
    landed_in(r2_land.at[:, pl.ds(0, 64)], pair_r.at[5])
    for side, out in ((0, dk_out), (1, dv_out)):
        terms = jnp.concatenate([r2_land[side], gg[side], d_l1[side]], axis=0)
        out[...] = (d_loc[side] + mm(to_rows[...], terms)).astype(BF)
        stores[2 + side].start()

    landed_in(lo_land, mp_r.at[1])
    lo_out[...] = (mine + lo_land[...].astype(F32)).astype(BF)
    stores[0].start()

    landed_in(gw_all.at[1 - core, pl.ds(0, 8)], pair_r.at[6])
    landed_in(gw_all.at[1 - core, pl.ds(0, 8)], pair_r.at[7])
    stores[4].start()

    landed_in(ug.at[pl.ds(0, NEAR - 1)], f1_s.at[0])
    landed_in(far.at[core, pl.ds(64, 128)], f1_s.at[1])
    landed_in(far.at[core, pl.ds(192, 192)], f2_s.at[0])
    landed_in(far_f32, f2_s.at[1])
    landed_in(r1_land, r1_s.at[0])
    landed_in(r1_f32, r1_s.at[1])
    landed_in(msg, r2_s.at[0])
    landed_in(gw_land.at[pl.ds(0, FAR - 1)], gw_s.at[0])
    landed_in(gw_ar.at[pl.ds(0, 3)], gw_s.at[1])
    landed_in(gw_land.at[pl.ds(0, FAR - 1)], gw_s.at[2])
    landed_in(msg0, pair_s.at[0])
    landed_in(msg, pair_s.at[1])
    landed_in(far.at[core, pl.ds(192, 256)], pair_s.at[2])
    landed_in(gw_x, pair_s.at[3])
    landed_in(d_land, pair_s.at[4])
    landed_in(msg0, pair_s.at[5])
    landed_in(gw_all.at[core, pl.ds(0, 8)], pair_s.at[6])
    landed_in(gw_all.at[core, pl.ds(0, 8)], pair_s.at[7])
    to_mp.wait_send()
    to_lo.wait_send()
    for store in stores:
        store.wait()


def hand_over(*refs):
    given, out, held, whole, sem = refs[0:5], refs[5:10], refs[10:15], refs[15], refs[16]
    first = [pltpu.make_async_copy(given[n], held[n], sem.at[n]) for n in range(4)]
    halves = [pltpu.make_async_copy(given[4].at[n], held[4].at[n], sem.at[8 + n]) for n in range(2)]
    second = [pltpu.make_async_copy(held[n], out[n], sem.at[4 + n]) for n in range(4)]
    for copy in halves + first:
        copy.start()
    for side in range(2):
        halves[side].wait()
        for f in range(FAR):
            part = held[4][side, f].astype(F32)
            for c in range(3):
                at = side * 384 + c * 128
                whole[CHUNK * f:CHUNK * f + CHUNK, at:at + 128] = part[c * CHUNK:c * CHUNK + CHUNK]
        columns = pl.ds(side * 384, 384)
        second.append(pltpu.make_async_copy(whole.at[:, columns], out[4].at[:, columns], sem.at[10 + side]))
        second[-1].start()
    for n in range(4):
        first[n].wait()
        second[n].start()
    for copy in second:
        copy.wait()


def on_device(query_rows, key_rows, value_rows, w_output, grad_output):
    vm = pltpu.VMEM
    dma = pltpu.SemaphoreType.DMA
    piece = (80, 128)
    scratch = [
        vm((256, 384), BF), vm((256, 384), BF), vm((256, 384), BF), vm((256, 384), BF),
        vm((256, 384), BF), vm((256, 384), BF), vm((256, 384), BF), vm((384, 768), BF), vm((256, 384), BF),
        vm((6, 256, 128), F32),
        vm((6, 16, 128), F32),
        vm((3, 128, KEYS), BF),
        vm((64, 256), BF),
        vm((192, 64), BF),
        vm((256, 320), BF),
        vm((3, 2, 128, 192), BF),
        vm((3, 2, 128, 192), BF),
        vm((2, 128, 384), BF),
        vm((2, 128, 384), BF),
        vm((2, KEYS, 384), BF),
        vm((64, 384), F32),
        vm((NEAR, 16, 384), BF),
        vm((112, 384), BF),
        vm((8, 384), F32),
        vm((2, 256, 384), BF),
        vm((3, 512, 128), BF),
        vm((3, 512, 128), BF),
        vm((3, KEYS + 192, 512), F32),
        vm((384, 256), BF),
        vm((384, 256), F32),
        vm((2, KEYS, 384), F32),
        vm((2, 384, 384), BF),
        vm((384, 384), BF),
        vm((128, 384), F32),
        vm((192, 384), BF),
        vm((64, 384), F32),
        vm((192, 384), BF),
        vm((64, 384), F32),
        vm((2, 64, 384), BF),
        vm((2, 64, 384), BF),
        vm((128, 384), BF),
        vm((2, 128, 384), BF),
        vm((2, 256, 384), F32),
        vm((2, 128, 384), BF),
        vm((FAR,) + piece, BF),
        vm((FAR,) + piece, BF),
        vm((FAR,) + piece, F32),
        vm((FAR,) + piece, BF),
        vm((FAR,) + piece, BF),
        vm(piece, BF),
        vm((4,) + piece, BF),
        vm((2, FAR) + piece, BF),
        vm((256, 384), BF),
        vm((256, 384), BF),
        dma((5,)),
        dma((5,)),
        dma((2,)), dma((2,)),
        dma((2,)), dma((2,)),
        dma((2,)), dma((2,)),
        dma((1,)), dma((1,)),
        dma((3,)), dma((4,)),
        dma((8,)), dma((8,)),
        dma((2,)), dma((2,)),
    ]
    rows = jax.ShapeDtypeStruct((256, 384), BF)
    chunks = jax.ShapeDtypeStruct((2, FAR) + piece, BF)
    in_hbm = pl.BlockSpec(memory_space=pltpu.HBM)
    results = pl.pallas_call(
        kernel,
        out_shape=(rows, rows, rows, rows, chunks),
        in_specs=[in_hbm] * 5,
        out_specs=(in_hbm,) * 5,
        scratch_shapes=scratch,
        compiler_params=pltpu.CompilerParams(
            collective_id=0, has_side_effects=True, vmem_limit_bytes=58 * 1024 * 1024),
        cost_estimate=pl.CostEstimate(flops=1_200_000_000, bytes_accessed=4_000_000, transcendentals=1_000_000),
    )(query_rows, key_rows, value_rows, w_output, grad_output)
    held = [vm((256, 384), BF)] * 4 + [vm((2, FAR) + piece, BF), vm((384, 768), F32)]
    return pl.pallas_call(
        hand_over,
        out_shape=(rows, rows, rows, rows, jax.ShapeDtypeStruct((384, 768), F32)),
        in_specs=[in_hbm] * 5,
        out_specs=(in_hbm,) * 5,
        scratch_shapes=held + [dma((12,))],
        compiler_params=pltpu.CompilerParams(vmem_limit_bytes=58 * 1024 * 1024),
    )(*results)


def solution(mesh):
    placed = (P("ctx", "mp"), P("ctx", "mp"), P("ctx", "mp"), P("mp", None), P("ctx", "mp"))
    return jax.shard_map(
        on_device,
        mesh=mesh,
        in_specs=placed,
        out_specs=(P("ctx", "mp"), P("ctx", "mp"), P("ctx", "mp"), P("ctx", "mp"), P("mp", None)),
        check_vma=False,
    )
```
